256 devices in a mesh: ctx: 64 (over x, z, core), ch: 4 (over y).
Axes of the slice: x: 4, y: 4, z: 8, core: 2. Of those that a mesh axis runs over, the one named last changes fastest.
Arguments:
- query_mr: bfloat16 [8192, 8192], P('ch', 'ctx'), may hold values from -18 to 18
- key_mr: bfloat16 [8192, 8192], P('ch', 'ctx'), may hold values from -6 to 6
- value_mr: bfloat16 [8192, 8192], P('ch', 'ctx'), may hold values from -6 to 6
- key_li: bfloat16 [8192, 8192], P('ch', 'ctx'), may hold values from -6 to 6
- cotangent: bfloat16 [8192, 8192], P('ch', 'ctx'), may hold values from -6 to 6
- norm_gain: float32 [8192], P('ch'), may hold values from 0.5 to 1.5
- filter_mr: float32 [8192, 128], P('ch'), may hold values from -0.5 to 0.5
- filter_li: float32 [8192, 8192], P('ch', 'ctx'), may hold values from -1 to 1
Outputs:
- grad_query: bfloat16 [8192, 8192], P('ch', 'ctx')
- grad_key: bfloat16 [8192, 8192], P('ch', 'ctx')
- grad_value: bfloat16 [8192, 8192], P('ch', 'ctx')
- grad_key_li: bfloat16 [8192, 8192], P('ch', 'ctx')
- grad_gain: float32 [8192], P('ch')
- grad_filter_mr: float32 [8192, 128], P('ch')
- grad_filter_li: float32 [8192, 8192], P('ch', 'ctx')
The draws below stay inside these ranges and needn't reach their ends.
All inputs are finite; a program needn't handle non-finite values.
Results may differ from the reference program's by a relative error of at most 0.0085.
Values may be sent and summed in bfloat16 or wider, within the bound.
No kernel may reach another device: no remote copies, remote signals or barrier semaphores. Data moves between devices by JAX's collectives and lax.ppermute only.
A program may use at most 128 MiB of HBM per device.

```python
import jax
import jax.numpy as jnp
from jax import lax

D = 8192
TAPS = 128
LENGTH = 8192
N_CTX = 64
N_CH = 4


def draw_query_mr(key, part):
    key = jax.random.fold_in(key, 11)
    first, second = jax.random.split(key)
    rising = 3.0 ** (jnp.arange(D, dtype=jnp.float32) / D)
    spread_factor = jax.random.uniform(second, (D, 1), jnp.float32, 0.5, 1.5)
    values = jnp.clip(jax.random.normal(first, (D, LENGTH), jnp.float32), -4.0, 4.0)
    return (values * rising[:, None] * spread_factor).astype(jnp.bfloat16)


def draw_filter_li(key, part):
    key = jax.random.fold_in(key, 23)
    first, second = jax.random.split(key)
    low = jnp.log(0.3 / LENGTH)
    high = jnp.log(1.0 / 40.0)
    rates = jnp.exp(jax.random.uniform(second, (D, 1), jnp.float32, low, high))
    steps_along = jnp.arange(LENGTH, dtype=jnp.float32)[None, :]
    noise = jnp.clip(jax.random.normal(first, (D, LENGTH), jnp.float32), -4.0, 4.0)
    return noise * jnp.sqrt(2.0 * rates) * jnp.exp(-rates * steps_along)


def shard_levels(key, shape, cuts, low, top_value):
    factor_of = 1.0
    for axis_at, parts in cuts:
        steps = jax.random.uniform(jax.random.fold_in(jax.random.fold_in(key, 6), axis_at), (parts,), jnp.float32, low / len(cuts), top_value / len(cuts))
        factor_of = factor_of * jnp.repeat(jnp.exp(steps), shape[axis_at] // parts).reshape((-1,) + (1,) * (len(shape) - 1 - axis_at))
    return factor_of


def scatter_about(key, extent, spread, bound, cuts=(), kind=jnp.bfloat16):
    entries = spread * jax.random.normal(key, extent, jnp.float32)
    if cuts:
        entries = entries * shard_levels(key, extent, cuts, -0.22, 0.18)
    return jnp.clip(entries, -bound, bound).astype(kind)


def setup_inputs(seed: int = 0) -> dict:
    splits = jax.random.split(jax.random.key(seed), 9)
    return {
        "query_mr": draw_query_mr(jax.random.fold_in(splits[8], 71), 0),
        "key_mr": scatter_about(splits[1], (D, LENGTH), 1.0, 6.0, ((0, 4), (1, 64))),
        "value_mr": scatter_about(splits[2], (D, LENGTH), 1.0, 6.0, ((0, 4), (1, 64))),
        "key_li": scatter_about(splits[3], (D, LENGTH), 1.0, 6.0, ((0, 4), (1, 64))),
        "cotangent": scatter_about(splits[4], (D, LENGTH), 1.0, 6.0, ((0, 4), (1, 64))),
        "norm_gain": jnp.clip(1.0 + 0.1 * jax.random.normal(splits[5], (D,), jnp.float32), 0.5, 1.5),
        "filter_mr": scatter_about(splits[6], (D, TAPS), TAPS ** -0.5, 0.5, ((0, 4),), jnp.float32),
        "filter_li": draw_filter_li(jax.random.fold_in(splits[8], 71), 0),
    }


EPSILON = 1e-06
HIGHEST = lax.Precision.HIGHEST

def causal_filter(padded, taps):
    count = taps.shape[1]
    out_len = padded.shape[1] - count + 1

    def add_tap(index, total):
        piece = lax.dynamic_slice_in_dim(padded, count - 1 - index, out_len, 1)
        return total + lax.dynamic_slice_in_dim(taps, index, 1, 1) * piece
    return lax.fori_loop(0, count, add_tap, jnp.zeros((padded.shape[0], out_len), padded.dtype))

def later_filter(padded, taps):
    count = taps.shape[1]
    out_len = padded.shape[1] - count + 1

    def add_tap(index, total):
        piece = lax.dynamic_slice_in_dim(padded, index, out_len, 1)
        return total + lax.dynamic_slice_in_dim(taps, index, 1, 1) * piece
    return lax.fori_loop(0, count, add_tap, jnp.zeros((padded.shape[0], out_len), padded.dtype))

def tap_gradient(padded, grads):
    out_len = grads.shape[1]
    count = padded.shape[1] - out_len + 1

    def one_tap(index):
        piece = lax.dynamic_slice_in_dim(padded, count - 1 - index, out_len, 1)
        return lax.optimization_barrier(jnp.sum(grads * piece, axis=1))
    columns = lax.map(one_tap, jnp.arange(count, dtype=jnp.int32))
    return columns.T

def rounded(values):
    return lax.optimization_barrier(values.astype(jnp.bfloat16))

def spectral(pieces):
    signal, cotan, filt = pieces
    total = 2 * LENGTH
    signal_hat = jnp.fft.rfft(signal.astype(jnp.float32), n=total, axis=-1)
    cotan_hat = jnp.fft.rfft(cotan.astype(jnp.float32), n=total, axis=-1)
    filter_hat = jnp.fft.rfft(filt, n=total, axis=-1)
    back = jnp.fft.irfft(cotan_hat * jnp.conj(filter_hat), n=total, axis=-1)[:, :LENGTH]
    fgrad = jnp.fft.irfft(cotan_hat * jnp.conj(signal_hat), n=total, axis=-1)[:, :LENGTH]
    return (back.astype(jnp.bfloat16), fgrad.astype(jnp.float32))

def reference(query_mr, key_mr, value_mr, key_li, cotangent, norm_gain, filter_mr, filter_li):
    query = query_mr.astype(jnp.float32)
    key_f = key_mr.astype(jnp.float32)
    value_f = value_mr.astype(jnp.float32)
    keyli_f = key_li.astype(jnp.float32)
    product = key_f * value_f
    padded = jnp.pad(product, ((0, 0), (TAPS - 1, 0)))
    conv_out = causal_filter(padded, filter_mr)
    mixed = rounded(query * conv_out).astype(jnp.float32)
    inv_rms = lax.rsqrt(lax.optimization_barrier(jnp.sum(mixed * mixed, axis=0)) / D + EPSILON)
    normed = mixed * inv_rms
    scaled = normed * norm_gain[:, None]
    signal = (scaled * keyli_f).astype(jnp.bfloat16)
    blocks = N_CH * N_CTX
    grad_signal, grad_filter_li = lax.map(spectral, (signal.reshape(blocks, -1, LENGTH), cotangent.reshape(blocks, -1, LENGTH), filter_li.reshape(blocks, -1, LENGTH)))
    grad_signal = grad_signal.reshape(D, LENGTH).astype(jnp.float32)
    grad_filter_li = grad_filter_li.reshape(D, LENGTH)
    grad_scaled = grad_signal * keyli_f
    grad_key_li = (grad_signal * scaled).astype(jnp.bfloat16)
    grad_gain = lax.optimization_barrier(jnp.sum(grad_scaled * normed, axis=1))
    grad_normed = grad_scaled * norm_gain[:, None]
    project = lax.optimization_barrier(jnp.sum(grad_normed * normed, axis=0)) / D
    grad_mixed = inv_rms * (grad_normed - normed * project)
    grad_query = (grad_mixed * conv_out).astype(jnp.bfloat16)
    grad_conv = grad_mixed * query
    later = jnp.pad(grad_conv, ((0, 0), (0, TAPS - 1)))
    grad_product = later_filter(later, filter_mr)
    grad_key = (grad_product * value_f).astype(jnp.bfloat16)
    grad_value = (grad_product * key_f).astype(jnp.bfloat16)
    grad_filter_mr = tap_gradient(padded, grad_conv)
    return (grad_query, grad_key, grad_value, grad_key_li, grad_gain, grad_filter_mr, grad_filter_li)
```

```python
import functools
import math

import jax
import jax.numpy as jnp
import numpy as np
from jax import lax
from jax.experimental import pallas as pl
from jax.experimental.pallas import tpu as pltpu
from jax.sharding import PartitionSpec as P

D = 8192
LANES = 128
EPSILON = 1e-06
BF16 = jnp.bfloat16
F32 = jnp.float32


def halves(table):
    high = table.astype(np.float32).astype(BF16)
    low = (table - high.astype(np.float64)).astype(np.float32).astype(BF16)
    return jnp.asarray(high), jnp.asarray(low)


def short_tables():
    place = np.arange(2 * LANES)
    angle = 2.0 * math.pi / (2 * LANES) * place[:, None] * (np.arange(LANES)[None, :] + 0.5)
    ahead = np.concatenate([np.cos(angle), -np.sin(angle)], axis=1)
    return halves(ahead) + halves(ahead.T / LANES)


def long_tables(blocks):
    radix = 2 * blocks
    total = radix * LANES
    half = np.arange(blocks) + 0.5
    outer = 2.0 * math.pi / radix * half[:, None] * np.arange(blocks)[None, :]
    first = np.concatenate([np.cos(outer), -np.sin(outer)], axis=0)
    twist = 2.0 * math.pi / total * half[:, None] * np.arange(LANES)[None, :]
    inner = 2.0 * math.pi / LANES * (np.arange(LANES)[:, None] * np.arange(LANES)[None, :] % LANES)
    cosine, sine = np.cos(inner), np.sin(inner)
    second = np.block([[cosine, -sine], [sine, cosine]])
    first_high, first_low = halves(first)
    last_high, last_low = halves(first.T * (2.0 / total))
    return (
        jnp.concatenate([first_high, first_low], axis=1),
        jnp.asarray(np.cos(twist), F32),
        jnp.asarray(np.sin(twist), F32),
        *halves(second),
        *halves(second.T),
        jnp.concatenate([last_high, last_high, last_low], axis=1),
    )


def dot(left, right):
    return jnp.dot(left, right, preferred_element_type=F32)


def split(values):
    high = values.astype(BF16)
    return high, (values - high.astype(F32)).astype(BF16)


def dot3(values, high, low):
    values_high, values_low = split(values)
    return dot(values_high, high) + dot(values_low, high) + dot(values_high, low)


def mr_forward_kernel(
    key, value, prior, query, key_li, gain, taps, ahead_high, ahead_low, back_high, back_low,
    conv_out, mixed_out, scaled_out, gated_out, window_spec, taps_spec, squares,
):
    product = key[...].astype(F32) * value[...].astype(F32)
    window = jnp.concatenate([prior[...].astype(F32), product], axis=1)
    spec = dot3(window, ahead_high[...], ahead_low[...])
    filt = dot3(taps[...], ahead_high[:LANES], ahead_low[:LANES])
    spec_re, spec_im = spec[:, :LANES], spec[:, LANES:]
    filt_re, filt_im = filt[:, :LANES], filt[:, LANES:]
    passed = jnp.concatenate(
        [spec_re * filt_re - spec_im * filt_im, spec_re * filt_im + spec_im * filt_re], axis=1
    )
    conv = dot3(passed, back_high[:, LANES:], back_low[:, LANES:])
    mixed_bf = (query[...].astype(F32) * conv).astype(BF16)
    mixed = mixed_bf.astype(F32)
    gain_col = gain[...]
    conv_out[...] = conv
    mixed_out[...] = mixed_bf
    scaled_out[...] = mixed * gain_col
    gated_out[...] = key_li[...].astype(F32) * gain_col
    window_spec[...] = spec
    taps_spec[...] = filt

    @pl.when(pl.program_id(0) == 0)
    def _():
        squares[...] = jnp.zeros_like(squares)

    squares[...] += jnp.sum(mixed * mixed, axis=0, keepdims=True)


def mr_backward_kernel(
    grad_signal, gated, mixed, conv, query, inv_rms, project, window_spec, taps_spec,
    ahead_high, ahead_low, back_high, back_low,
    grad_query, taps_grad, before_grad, own_grad,
):
    inv = inv_rms[...]
    normed = mixed[...].astype(F32) * inv
    grad_mixed = inv * (grad_signal[...].astype(F32) * gated[...] - normed * project[...])
    grad_query[...] = (grad_mixed * conv[...]).astype(BF16)
    grad_conv = grad_mixed * query[...].astype(F32)
    spec = dot3(grad_conv, ahead_high[LANES:], ahead_low[LANES:])
    spec_re, spec_im = spec[:, :LANES], spec[:, LANES:]

    def against(other):
        other_re, other_im = other[:, :LANES], other[:, LANES:]
        return jnp.concatenate(
            [spec_re * other_re + spec_im * other_im, spec_im * other_re - spec_re * other_im],
            axis=1,
        )

    taps_grad[...] = dot3(
        against(window_spec[...]), back_high[:, :LANES], back_low[:, :LANES]
    ).astype(BF16)
    both = dot3(against(taps_spec[...]), back_high[...], back_low[...])
    before_grad[...] = both[:, :LANES].astype(BF16)
    own_grad[...] = both[:, LANES:]


ROWS = 256


def row_spec(width=LANES):
    return pl.BlockSpec((ROWS, width), lambda i: (i, 0))


def whole_spec(shape):
    return pl.BlockSpec(shape, lambda i: (0,) * len(shape))


def mr_forward(key, value, prior, query, key_li, gain, taps, tables):
    rows = key.shape[0]
    wide = jax.ShapeDtypeStruct((rows, 2 * LANES), F32)
    full = jax.ShapeDtypeStruct((rows, LANES), F32)
    half = jax.ShapeDtypeStruct((rows, LANES), BF16)
    return pl.pallas_call(
        mr_forward_kernel,
        grid=(rows // ROWS,),
        in_specs=[row_spec()] * 5
        + [row_spec(1), row_spec()]
        + [whole_spec(table.shape) for table in tables],
        out_specs=[row_spec()] * 4 + [row_spec(2 * LANES)] * 2 + [whole_spec((1, LANES))],
        out_shape=[full, half, full, full, wide, wide, jax.ShapeDtypeStruct((1, LANES), F32)],
        name="mr_forward",
    )(key, value, prior, query, key_li, gain, taps, *tables)


def mr_backward(
    grad_signal, gated, mixed, conv, query, inv_rms, project, window_spec, taps_spec, tables
):
    rows = mixed.shape[0]
    half = jax.ShapeDtypeStruct((rows, LANES), BF16)
    return pl.pallas_call(
        mr_backward_kernel,
        grid=(rows // ROWS,),
        in_specs=[row_spec()] * 5
        + [whole_spec((1, LANES))] * 2
        + [row_spec(2 * LANES)] * 2
        + [whole_spec(table.shape) for table in tables],
        out_specs=[row_spec()] * 4,
        out_shape=[half, half, half, jax.ShapeDtypeStruct((rows, LANES), F32)],
        name="mr_backward",
    )(grad_signal, gated, mixed, conv, query, inv_rms, project, window_spec, taps_spec, *tables)


GROUP = 4


def channel_rows(channel, blocks, width):
    return pl.ds(channel, blocks, stride=width)


def to_spectrum(flat, channels, blocks, width, first, cosine, sine, high, low):
    pieces = [flat[channel_rows(c, blocks, width), :].astype(BF16) for c in channels]
    grid = jnp.concatenate(pieces, axis=1)
    outer = dot(first[...], jnp.concatenate([grid, grid], axis=0))
    cos, sin = cosine[...], sine[...]
    turned = []
    for at in range(len(channels)):
        lanes = slice(at * LANES, (at + 1) * LANES)
        real, imag = outer[:blocks, lanes], outer[blocks:, lanes]
        turned.append(
            jnp.concatenate([real * cos + imag * sin, imag * cos - real * sin], axis=1)
        )
    return dot3(jnp.concatenate(turned, axis=0), high[...], low[...])


def from_spectrum(spec, count, blocks, high, low, cosine, sine, last):
    inner = dot3(spec, high[...], low[...])
    cos, sin = cosine[...], sine[...]
    turned = []
    for at in range(count):
        rows = slice(at * blocks, (at + 1) * blocks)
        real, imag = inner[rows, :LANES], inner[rows, LANES:]
        turned.append(
            jnp.concatenate([real * cos - imag * sin, imag * cos + real * sin], axis=0)
        )
    top, rest = split(jnp.concatenate(turned, axis=1))
    return dot(last[...], jnp.concatenate([top, rest, top], axis=0))


def times_conj(left, right):
    left_re, left_im = left[:, :LANES], left[:, LANES:]
    right_re, right_im = right[:, :LANES], right[:, LANES:]
    return jnp.concatenate(
        [left_re * right_re + left_im * right_im, left_im * right_re - left_re * right_im], axis=1
    )


def signal_grad_kernel(
    blocks, width, cotan, filt, first, cosine, sine, high, low, back_high, back_low, last,
    grad_out, cotan_spec, cotan_flat, filt_flat, grad_flat,
):
    cotan_flat[...] = cotan[...].astype(F32)
    filt_flat[...] = filt[...].astype(F32)

    def one_group(step, carry):
        channels = [step * GROUP + at for at in range(GROUP)]
        spectrum = functools.partial(
            to_spectrum, channels=channels, blocks=blocks, width=width,
            first=first, cosine=cosine, sine=sine, high=high, low=low,
        )
        moved = spectrum(cotan_flat)
        rows = pl.ds(pl.multiple_of(step * (GROUP * blocks), GROUP * blocks), GROUP * blocks)
        cotan_spec[rows, :] = moved
        grads = from_spectrum(
            times_conj(moved, spectrum(filt_flat)),
            GROUP, blocks, back_high, back_low, cosine, sine, last,
        )
        for at, channel in enumerate(channels):
            lanes = slice(at * LANES, (at + 1) * LANES)
            grad_flat[channel_rows(channel, blocks, width), :] = grads[:, lanes]
        return carry

    lax.fori_loop(0, width // GROUP, one_group, 0)
    grad_out[...] = grad_flat[...].astype(BF16)


def filter_grad_kernel(
    blocks, width, signal, cotan_spec, grad_signal, first, cosine, sine, high, low, back_high,
    back_low, last, grad_out, gain_terms, signal_flat, grad_flat,
):
    signal_flat[...] = signal[...].astype(F32)
    terms = signal_flat[...] * grad_signal[...].astype(F32)
    gain_terms[...] = jnp.sum(terms.reshape(blocks, width, LANES), axis=0)

    def one_group(step, carry):
        channels = [step * GROUP + at for at in range(GROUP)]
        moved = to_spectrum(
            signal_flat, channels, blocks, width, first, cosine, sine, high, low
        )
        rows = pl.ds(pl.multiple_of(step * (GROUP * blocks), GROUP * blocks), GROUP * blocks)
        grads = from_spectrum(
            times_conj(cotan_spec[rows, :], moved),
            GROUP, blocks, back_high, back_low, cosine, sine, last,
        )
        for at, channel in enumerate(channels):
            lanes = slice(at * LANES, (at + 1) * LANES)
            grad_flat[channel_rows(channel, blocks, width), :] = grads[:, lanes]
        return carry

    lax.fori_loop(0, width // GROUP, one_group, 0)
    grad_out[...] = grad_flat[...].astype(BF16)


VMEM = pl.BlockSpec(memory_space=pltpu.VMEM)
LIMIT = pltpu.CompilerParams(vmem_limit_bytes=48 * 1024 * 1024)


def signal_grad(cotan, filt, blocks, tables):
    rows = cotan.shape[0]
    flat = pltpu.VMEM((rows, LANES), F32)
    return pl.pallas_call(
        functools.partial(signal_grad_kernel, blocks, rows // blocks),
        in_specs=[VMEM] * (2 + len(tables)),
        out_specs=[VMEM] * 2,
        out_shape=[
            jax.ShapeDtypeStruct((rows, LANES), BF16),
            jax.ShapeDtypeStruct((rows, 2 * LANES), F32),
        ],
        scratch_shapes=[flat] * 3,
        compiler_params=LIMIT,
        name="signal_grad",
    )(cotan, filt, *tables)


def filter_grad(signal, cotan_spec, grad_signal, blocks, tables):
    rows = signal.shape[0]
    flat = pltpu.VMEM((rows, LANES), F32)
    return pl.pallas_call(
        functools.partial(filter_grad_kernel, blocks, rows // blocks),
        in_specs=[VMEM] * (3 + len(tables)),
        out_specs=[VMEM] * 2,
        out_shape=[
            jax.ShapeDtypeStruct((rows, LANES), BF16),
            jax.ShapeDtypeStruct((rows // blocks, LANES), F32),
        ],
        scratch_shapes=[flat] * 2,
        compiler_params=LIMIT,
        name="filter_grad",
    )(signal, cotan_spec, grad_signal, *tables)


def swapped(rows):
    return lax.all_to_all(rows, "ctx", split_axis=0, concat_axis=0, tiled=True)


def shifted(block, distance):
    devices = range(lax.axis_size("ctx"))
    route = [(i - distance, i) for i in devices if i - distance in devices]
    return lax.ppermute(block, "ctx", route)


def local(query_mr, key_mr, value_mr, key_li, cotangent, norm_gain, filter_mr, filter_li):
    blocks = lax.axis_size("ctx")
    rows = query_mr.shape[0]
    short = short_tables()
    long = long_tables(blocks)
    product = (key_mr.astype(F32) * value_mr.astype(F32)).astype(BF16)
    prior = shifted(product, 1)
    moved_cotan = swapped(cotangent)
    moved_filter = swapped(filter_li.astype(BF16))
    conv, mixed, scaled, gated, window_spec, taps_spec, squares = mr_forward(
        key_mr, value_mr, prior, query_mr, key_li, norm_gain[:, None], filter_mr, short
    )
    inv_rms = lax.rsqrt(lax.psum(squares, "ch") / D + EPSILON)
    signal = (scaled * inv_rms * key_li.astype(F32)).astype(BF16)
    moved_signal = swapped(signal)
    grad_moved, cotan_spec = signal_grad(moved_cotan, moved_filter, blocks, long)
    grad_signal = swapped(grad_moved)
    filter_grad_moved, gain_terms = filter_grad(
        moved_signal, cotan_spec, grad_moved, blocks, long
    )
    grad_filter_li = swapped(filter_grad_moved).astype(F32)

    grad_f = grad_signal.astype(F32)
    grad_key_li = (grad_f * (scaled * inv_rms)).astype(BF16)
    project = lax.psum(
        jnp.sum(grad_f * gated * (mixed.astype(F32) * inv_rms), axis=0, keepdims=True), "ch"
    )
    grad_query, taps_grad, before_grad, own_grad = mr_backward(
        grad_signal, gated, mixed, conv, query_mr, inv_rms, project / D, window_spec, taps_spec,
        short,
    )
    after = shifted(before_grad, -1)
    grad_product = own_grad + after.astype(F32)
    grad_key = (grad_product * value_mr.astype(F32)).astype(BF16)
    grad_value = (grad_product * key_mr.astype(F32)).astype(BF16)

    taps_sum = jnp.sum(swapped(taps_grad).reshape(blocks, -1, LANES).astype(F32), axis=0)
    gain_sum = jnp.sum(gain_terms, axis=1).reshape(1, -1)
    gain_row = jnp.pad(gain_sum, ((0, 7), (0, LANES - gain_sum.shape[1])))
    gathered = lax.all_gather(
        jnp.concatenate([taps_sum, gain_row], axis=0), "ctx", axis=0, tiled=False
    )
    width = rows // blocks
    grad_filter_mr = gathered[:, :width].reshape(rows, LANES)
    grad_gain = gathered[:, width, :width].reshape(rows) / norm_gain
    return (
        grad_query,
        grad_key,
        grad_value,
        grad_key_li,
        grad_gain,
        grad_filter_mr,
        grad_filter_li,
    )


def solution(mesh):
    in_specs = (
        P("ch", "ctx"),
        P("ch", "ctx"),
        P("ch", "ctx"),
        P("ch", "ctx"),
        P("ch", "ctx"),
        P("ch"),
        P("ch", None),
        P("ch", "ctx"),
    )
    out_specs = (
        P("ch", "ctx"),
        P("ch", "ctx"),
        P("ch", "ctx"),
        P("ch", "ctx"),
        P("ch"),
        P("ch", None),
        P("ch", "ctx"),
    )
    return jax.shard_map(local, mesh=mesh, in_specs=in_specs, out_specs=out_specs, check_vma=False)
```

```python
import functools
import math

import jax
import jax.numpy as jnp
import numpy as np
from jax import lax
from jax.experimental import pallas as pl
from jax.experimental.pallas import tpu as pltpu
from jax.sharding import PartitionSpec as P

D = 8192
LANES = 128
EPSILON = 1e-06
BF16 = jnp.bfloat16
F32 = jnp.float32


def halves(table):
    high = table.astype(np.float32).astype(BF16)
    low = (table - high.astype(np.float64)).astype(np.float32).astype(BF16)
    return jnp.asarray(high), jnp.asarray(low)


def short_tables():
    place = np.arange(2 * LANES)
    angle = 2.0 * math.pi / (2 * LANES) * place[:, None] * (np.arange(LANES)[None, :] + 0.5)
    ahead = np.concatenate([np.cos(angle), -np.sin(angle)], axis=1)
    return halves(ahead) + halves(ahead.T / LANES)


def long_tables(blocks):
    radix = 2 * blocks
    total = radix * LANES
    half = np.arange(blocks) + 0.5
    outer = 2.0 * math.pi / radix * half[:, None] * np.arange(blocks)[None, :]
    first = np.concatenate([np.cos(outer), -np.sin(outer)], axis=0)
    twist = 2.0 * math.pi / total * half[:, None] * np.arange(LANES)[None, :]
    inner = 2.0 * math.pi / LANES * (np.arange(LANES)[:, None] * np.arange(LANES)[None, :] % LANES)
    cosine, sine = np.cos(inner), np.sin(inner)
    second = np.block([[cosine, -sine], [sine, cosine]])
    first_high, first_low = halves(first)
    last_high, last_low = halves(first.T * (2.0 / total))
    return (
        jnp.concatenate([first_high, first_low], axis=1),
        jnp.asarray(np.cos(twist), F32),
        jnp.asarray(np.sin(twist), F32),
        *halves(second),
        *halves(second.T),
        jnp.concatenate([last_high, last_high, last_low], axis=1),
    )


def dot(left, right):
    return jnp.dot(left, right, preferred_element_type=F32)


def split(values):
    high = values.astype(BF16)
    return high, (values - high.astype(F32)).astype(BF16)


def dot3(values, high, low):
    values_high, values_low = split(values)
    return dot(
        jnp.concatenate([values_high, values_low, values_high], axis=1),
        jnp.concatenate([high, high, low], axis=0),
    )


def product_kernel(key, value, product):
    product[...] = (key[...].astype(F32) * value[...].astype(F32)).astype(BF16)


def pair_kernel(cotan, filt, unread, pair):
    blocks, both = pair.shape[:2]
    pair[:, : both // 2, :] = cotan[...].reshape(blocks, -1, LANES)
    pair[:, both // 2 :, :] = filt[...].astype(BF16).reshape(blocks, -1, LANES)


def gain_column(gain):
    here = lax.broadcasted_iota(jnp.int32, (LANES, LANES), 0)
    diagonal = here == lax.broadcasted_iota(jnp.int32, (LANES, LANES), 1)
    columns = [
        jnp.sum(jnp.where(diagonal, gain[at : at + 1, :], 0.0), axis=1, keepdims=True)
        for at in range(gain.shape[0])
    ]
    return jnp.concatenate(columns, axis=0)


def mr_forward_kernel(
    key, value, prior, query, taps, unread, ahead_high, ahead_low, back_high, back_low,
    conv_out, mixed_out, window_spec, taps_spec, squares,
):
    product = key[...].astype(F32) * value[...].astype(F32)
    window = jnp.concatenate([prior[...].astype(F32), product], axis=1)
    spec = dot3(window, ahead_high[...], ahead_low[...])
    filt = dot3(taps[...], ahead_high[:LANES], ahead_low[:LANES])
    spec_re, spec_im = spec[:, :LANES], spec[:, LANES:]
    filt_re, filt_im = filt[:, :LANES], filt[:, LANES:]
    passed = jnp.concatenate(
        [spec_re * filt_re - spec_im * filt_im, spec_re * filt_im + spec_im * filt_re], axis=1
    )
    conv = dot3(passed, back_high[:, LANES:], back_low[:, LANES:])
    mixed_bf = (query[...].astype(F32) * conv).astype(BF16)
    mixed = mixed_bf.astype(F32)
    conv_out[...] = conv
    mixed_out[...] = mixed_bf
    window_spec[...] = spec
    taps_spec[...] = filt

    @pl.when(pl.program_id(0) == 0)
    def _():
        squares[...] = jnp.zeros_like(squares)

    squares[...] += jnp.sum(mixed * mixed, axis=0, keepdims=True)


def gain_block(gain, count):
    groups = count // LANES
    return gain_column(gain[pl.ds(pl.program_id(0) * groups, groups), :])


def total(parts):
    return functools.reduce(lambda left, right: left + right, [part[...] for part in parts])


def gate_kernel(mixed, key_li, gain, *rest):
    squares, signal, inv_out = rest[:-2], rest[-2], rest[-1]
    inv = lax.rsqrt(total(squares) / D + EPSILON)
    inv_out[...] = inv
    scaled = mixed[...].astype(F32) * inv * gain_block(gain, mixed.shape[0])
    signal[...] = (scaled * key_li[...].astype(F32)).astype(BF16)


def mr_project_kernel(grad_signal, key_li, mixed, gain, inv_rms, grad_key_li, project):
    grad = grad_signal[...].astype(F32)
    scaled = mixed[...].astype(F32) * inv_rms[...] * gain_block(gain, mixed.shape[0])
    grad_scaled = grad * scaled
    grad_key_li[...] = grad_scaled.astype(BF16)

    @pl.when(pl.program_id(0) == 0)
    def _():
        project[...] = jnp.zeros_like(project)

    project[...] += jnp.sum(grad_scaled * key_li[...].astype(F32), axis=0, keepdims=True)


def mr_backward_kernel(
    grad_signal, key_li, mixed, conv, query, gain, inv_rms, window_spec, taps_spec,
    ahead_high, ahead_low, back_high, back_low, *rest,
):
    project = total(rest[:-4]) / D
    grad_query, taps_grad, before_grad, own_grad = rest[-4:]
    inv = inv_rms[...]
    normed = mixed[...].astype(F32) * inv
    gated = key_li[...].astype(F32) * gain_block(gain, mixed.shape[0])
    grad_mixed = inv * (grad_signal[...].astype(F32) * gated - normed * project)
    grad_query[...] = (grad_mixed * conv[...]).astype(BF16)
    grad_conv = grad_mixed * query[...].astype(F32)
    spec = dot3(grad_conv, ahead_high[LANES:], ahead_low[LANES:])
    spec_re, spec_im = spec[:, :LANES], spec[:, LANES:]

    def against(other):
        other_re, other_im = other[:, :LANES], other[:, LANES:]
        return jnp.concatenate(
            [spec_re * other_re + spec_im * other_im, spec_im * other_re - spec_re * other_im],
            axis=1,
        )

    taps_grad[...] = dot3(
        against(window_spec[...]), back_high[:, :LANES], back_low[:, :LANES]
    ).astype(BF16)
    both = dot3(against(taps_spec[...]), back_high[...], back_low[...])
    before_grad[...] = both[:, :LANES].astype(BF16)
    own_grad[...] = both[:, LANES:]


UNREAD = pl.BlockSpec(memory_space=pl.ANY)
LIMIT = pltpu.CompilerParams(vmem_limit_bytes=60 * 1024 * 1024)
PRODUCT_ROWS = 1024
PAIR_ROWS = 1024
FORWARD_ROWS = 1024
GATE_ROWS = 1024
PROJECT_ROWS = 1024
BACKWARD_ROWS = 1024


def row_spec(count, width=LANES):
    return pl.BlockSpec((count, width), lambda i: (i, 0))


def whole_spec(shape):
    return pl.BlockSpec(shape, lambda i: (0,) * len(shape))


def by_rows(kernel, name, count, rows, ins, in_specs, outs, out_specs):
    return pl.pallas_call(
        kernel,
        grid=(rows // count,),
        in_specs=in_specs,
        out_specs=out_specs,
        out_shape=[jax.ShapeDtypeStruct(*out) for out in outs],
        compiler_params=LIMIT,
        name=name,
    )(*ins)


ROW = ((1, LANES), F32)


def product_of(key, value):
    rows = key.shape[0]
    each = row_spec(PRODUCT_ROWS)
    return by_rows(
        product_kernel, "product_of", PRODUCT_ROWS, rows,
        (key, value), [each] * 2, [((rows, LANES), BF16)], [each],
    )[0]


def pair_up(cotan, filt, after, blocks):
    rows = cotan.shape[0]
    width = rows // blocks
    return by_rows(
        pair_kernel, "pair_up", PAIR_ROWS, rows,
        (cotan, filt, after), [row_spec(PAIR_ROWS)] * 2 + [UNREAD],
        [((blocks, 2 * width, LANES), BF16)],
        [pl.BlockSpec((PAIR_ROWS // width, 2 * width, LANES), lambda i: (i, 0, 0))],
    )[0]


def mr_forward(key, value, prior, query, taps, after, tables):
    rows = key.shape[0]
    each, wide = row_spec(FORWARD_ROWS), row_spec(FORWARD_ROWS, 2 * LANES)
    return by_rows(
        mr_forward_kernel, "mr_forward", FORWARD_ROWS, rows,
        (key, value, prior, query, taps, after, *tables),
        [each] * 5 + [UNREAD] + [whole_spec(table.shape) for table in tables],
        [((rows, LANES), F32), ((rows, LANES), BF16)] + [((rows, 2 * LANES), F32)] * 2 + [ROW],
        [each, each, wide, wide, whole_spec((1, LANES))],
    )


def gate(mixed, key_li, gain, squares):
    rows = mixed.shape[0]
    each = row_spec(GATE_ROWS)
    return by_rows(
        gate_kernel, "gate", GATE_ROWS, rows,
        (mixed, key_li, gain, *squares),
        [each] * 2 + [whole_spec(gain.shape)] + [whole_spec((1, LANES))] * len(squares),
        [((rows, LANES), BF16), ROW],
        [each, whole_spec((1, LANES))],
    )


def mr_project(grad_signal, key_li, mixed, gain, inv_rms):
    rows = mixed.shape[0]
    each = row_spec(PROJECT_ROWS)
    return by_rows(
        mr_project_kernel, "mr_project", PROJECT_ROWS, rows,
        (grad_signal, key_li, mixed, gain, inv_rms),
        [each] * 3 + [whole_spec(gain.shape), whole_spec((1, LANES))],
        [((rows, LANES), BF16), ROW],
        [each, whole_spec((1, LANES))],
    )


def mr_backward(
    grad_signal, key_li, mixed, conv, query, gain, inv_rms, window_spec, taps_spec, tables, project
):
    rows = mixed.shape[0]
    each, wide = row_spec(BACKWARD_ROWS), row_spec(BACKWARD_ROWS, 2 * LANES)
    return by_rows(
        mr_backward_kernel, "mr_backward", BACKWARD_ROWS, rows,
        (
            grad_signal, key_li, mixed, conv, query, gain, inv_rms, window_spec, taps_spec,
            *tables, *project,
        ),
        [each] * 5
        + [whole_spec(gain.shape), whole_spec((1, LANES))]
        + [wide] * 2
        + [whole_spec(table.shape) for table in tables]
        + [whole_spec((1, LANES))] * len(project),
        [((rows, LANES), BF16)] * 3 + [((rows, LANES), F32)],
        [each] * 4,
    )


def bundle_kernel(blocks, filter_grad, taps_grad, gain_terms, bundled):
    width = gain_terms.shape[0]
    bundled[:, :width, :] = filter_grad[...].reshape(blocks, width, LANES)
    taps = jnp.sum(taps_grad[...].astype(F32).reshape(blocks, width, LANES), axis=0)
    bundled[:, width : 2 * width, :] = jnp.broadcast_to(
        taps.astype(BF16)[None], (blocks, width, LANES)
    )
    sums = jnp.sum(gain_terms[...], axis=1, keepdims=True)
    high = sums.astype(BF16).astype(F32)
    lane = lax.broadcasted_iota(jnp.int32, (width, LANES), 1)
    row = lax.broadcasted_iota(jnp.int32, (width, LANES), 0)
    placed = jnp.where(lane == row, high, jnp.where(lane == row + width, sums - high, 0.0))
    line = jnp.sum(placed, axis=0, keepdims=True)
    bundled[:, 2 * width :, :] = jnp.broadcast_to(
        line.astype(BF16)[None], (blocks, EXTRA, LANES)
    )


def bundle(filter_grad, taps_grad, gain_terms, blocks):
    width = gain_terms.shape[0]
    shape = (blocks, 2 * width + EXTRA, LANES)
    ins = (filter_grad, taps_grad, gain_terms)
    return by_rows(
        functools.partial(bundle_kernel, blocks), "bundle", 1, 1,
        ins, [whole_spec(value.shape) for value in ins], [(shape, BF16)], [whole_spec(shape)],
    )[0]


def deliver_kernel(bundled, gain, filter_grad, taps_grad, gain_grad):
    width = gain.shape[1]
    values = bundled[...].astype(F32)
    filter_grad[...] = values[:, :width, :].reshape(filter_grad.shape)
    taps_grad[...] = values[:, width : 2 * width, :].reshape(taps_grad.shape)
    sums = values[:, 2 * width, :]
    gain_grad[...] = (sums[:, :width] + sums[:, width : 2 * width]) / gain[...]


def deliver(bundled, gain):
    blocks, width = gain.shape
    each = min(16, blocks)
    rows = row_spec(each * width)
    small = pl.BlockSpec((each, width), lambda i: (i, 0))
    return by_rows(
        deliver_kernel, "deliver", each, blocks,
        (bundled, gain),
        [pl.BlockSpec((each,) + bundled.shape[1:], lambda i: (i, 0, 0)), small],
        [((blocks * width, LANES), F32)] * 2 + [((blocks, width), F32)],
        [rows, rows, small],
    )


EXTRA = 8
GROUP = 8


def channel_rows(channel, blocks, width):
    return pl.ds(channel, blocks, stride=width)


def to_spectrum(flat, channels, blocks, width, first, cosine, sine, high, low):
    pieces = [flat[channel_rows(c, blocks, width), :].astype(BF16) for c in channels]
    grid = jnp.concatenate(pieces, axis=1)
    outer = dot(first[...], jnp.concatenate([grid, grid], axis=0))
    cos, sin = cosine[...], sine[...]
    turned = []
    for at in range(len(channels)):
        lanes = slice(at * LANES, (at + 1) * LANES)
        real, imag = outer[:blocks, lanes], outer[blocks:, lanes]
        turned.append(
            jnp.concatenate([real * cos + imag * sin, imag * cos - real * sin], axis=1)
        )
    return dot3(jnp.concatenate(turned, axis=0), high[...], low[...])


def from_spectrum(spec, count, blocks, high, low, cosine, sine, last):
    inner = dot3(spec, high[...], low[...])
    cos, sin = cosine[...], sine[...]
    turned = []
    for at in range(count):
        rows = slice(at * blocks, (at + 1) * blocks)
        real, imag = inner[rows, :LANES], inner[rows, LANES:]
        turned.append(
            jnp.concatenate([real * cos - imag * sin, imag * cos + real * sin], axis=0)
        )
    top, rest = split(jnp.concatenate(turned, axis=1))
    return dot(last[...], jnp.concatenate([top, rest, top], axis=0))


def times_conj(left, right):
    left_re, left_im = left[:, :LANES], left[:, LANES:]
    right_re, right_im = right[:, :LANES], right[:, LANES:]
    return jnp.concatenate(
        [left_re * right_re + left_im * right_im, left_im * right_re - left_re * right_im], axis=1
    )


def signal_grad_kernel(
    blocks, width, pair, unread, first, cosine, sine, high, low, back_high, back_low, last,
    grad_out, cotan_spec, pair_flat, grad_flat,
):
    pair_flat[...] = pair[...].astype(F32)

    def one_group(step, carry):
        channels = [step * GROUP + at for at in range(GROUP)]
        spectrum = functools.partial(
            to_spectrum, pair_flat, blocks=blocks, width=2 * width,
            first=first, cosine=cosine, sine=sine, high=high, low=low,
        )
        moved = spectrum(channels)
        rows = pl.ds(pl.multiple_of(step * (GROUP * blocks), GROUP * blocks), GROUP * blocks)
        cotan_spec[rows, :] = moved
        grads = from_spectrum(
            times_conj(moved, spectrum([width + channel for channel in channels])),
            GROUP, blocks, back_high, back_low, cosine, sine, last,
        )
        for at, channel in enumerate(channels):
            lanes = slice(at * LANES, (at + 1) * LANES)
            grad_flat[channel_rows(channel, blocks, width), :] = grads[:, lanes]
        return carry

    lax.fori_loop(0, width // GROUP, one_group, 0)
    grad_out[...] = grad_flat[...].astype(BF16)


def filter_grad_kernel(
    blocks, width, signal, cotan_spec, grad_signal, unread, first, cosine, sine, high, low, back_high,
    back_low, last, grad_out, gain_terms, signal_flat, grad_flat,
):
    signal_flat[...] = signal[...].astype(F32)
    terms = signal_flat[...] * grad_signal[...].astype(F32)
    gain_terms[...] = jnp.sum(terms.reshape(blocks, width, LANES), axis=0)

    def one_group(step, carry):
        channels = [step * GROUP + at for at in range(GROUP)]
        moved = to_spectrum(
            signal_flat, channels, blocks, width, first, cosine, sine, high, low
        )
        rows = pl.ds(pl.multiple_of(step * (GROUP * blocks), GROUP * blocks), GROUP * blocks)
        grads = from_spectrum(
            times_conj(cotan_spec[rows, :], moved),
            GROUP, blocks, back_high, back_low, cosine, sine, last,
        )
        for at, channel in enumerate(channels):
            lanes = slice(at * LANES, (at + 1) * LANES)
            grad_flat[channel_rows(channel, blocks, width), :] = grads[:, lanes]
        return carry

    lax.fori_loop(0, width // GROUP, one_group, 0)
    grad_out[...] = grad_flat[...].astype(BF16)


def signal_grad(pair, after, blocks, tables):
    rows = pair.shape[0] // 2
    return pl.pallas_call(
        functools.partial(signal_grad_kernel, blocks, rows // blocks),
        grid=(1,),
        in_specs=[whole_spec(pair.shape), UNREAD] + [whole_spec(table.shape) for table in tables],
        out_specs=[whole_spec((rows, LANES)), whole_spec((rows, 2 * LANES))],
        out_shape=[
            jax.ShapeDtypeStruct((rows, LANES), BF16),
            jax.ShapeDtypeStruct((rows, 2 * LANES), F32),
        ],
        scratch_shapes=[pltpu.VMEM((2 * rows, LANES), F32), pltpu.VMEM((rows, LANES), F32)],
        compiler_params=LIMIT,
        name="signal_grad",
    )(pair, after, *tables)


def filter_grad(signal, cotan_spec, grad_signal, after, blocks, tables):
    rows = signal.shape[0]
    flat = pltpu.VMEM((rows, LANES), F32)
    return pl.pallas_call(
        functools.partial(filter_grad_kernel, blocks, rows // blocks),
        grid=(1,),
        in_specs=[whole_spec(value.shape) for value in (signal, cotan_spec, grad_signal)]
        + [UNREAD]
        + [whole_spec(table.shape) for table in tables],
        out_specs=[whole_spec((rows, LANES)), whole_spec((rows // blocks, LANES))],
        out_shape=[
            jax.ShapeDtypeStruct((rows, LANES), BF16),
            jax.ShapeDtypeStruct((rows // blocks, LANES), F32),
        ],
        scratch_shapes=[flat] * 2,
        compiler_params=LIMIT,
        name="filter_grad",
    )(signal, cotan_spec, grad_signal, after, *tables)


def swapped(rows):
    return lax.all_to_all(rows, "ctx", split_axis=0, concat_axis=0, tiled=True)


def parts_over_ch(row):
    count = lax.axis_size("ch")
    routes = [[(i, (i + step) % count) for i in range(count)] for step in range(1, count)]
    return [row] + [lax.ppermute(row, "ch", route) for route in routes]


def shifted(block, distance):
    devices = range(lax.axis_size("ctx"))
    route = [(i - distance, i) for i in devices if i - distance in devices]
    return lax.ppermute(block, "ctx", route)


def local(query_mr, key_mr, value_mr, key_li, cotangent, norm_gain, filter_mr, filter_li):
    blocks = lax.axis_size("ctx")
    rows = query_mr.shape[0]
    short = short_tables()
    long = long_tables(blocks)
    width = rows // blocks
    gain = norm_gain.reshape(-1, LANES)
    product = product_of(key_mr, value_mr)
    prior = shifted(product, 1)
    pair = pair_up(cotangent, filter_li, product, blocks)
    moved_pair = swapped(pair).reshape(2 * rows, LANES)
    grad_moved, cotan_spec = signal_grad(moved_pair, prior, blocks, long)
    grad_signal = swapped(grad_moved)
    conv, mixed, window_spec, taps_spec, squares = mr_forward(
        key_mr, value_mr, prior, query_mr, filter_mr, grad_moved, short
    )
    signal, inv_rms = gate(mixed, key_li, gain, parts_over_ch(squares))
    moved_signal = swapped(signal)
    grad_key_li, terms = mr_project(grad_signal, key_li, mixed, gain, inv_rms)
    grad_query, taps_grad, before_grad, own_grad = mr_backward(
        grad_signal, key_li, mixed, conv, query_mr, gain, inv_rms, window_spec, taps_spec, short,
        parts_over_ch(terms),
    )
    moved_taps = swapped(taps_grad)
    filter_grad_moved, gain_terms = filter_grad(
        moved_signal, cotan_spec, grad_moved, taps_grad, blocks, long
    )
    after = shifted(before_grad, -1)
    grad_product = own_grad + after.astype(F32)
    grad_key = (grad_product * value_mr.astype(F32)).astype(BF16)
    grad_value = (grad_product * key_mr.astype(F32)).astype(BF16)

    bundled = swapped(bundle(filter_grad_moved, moved_taps, gain_terms, blocks))
    grad_filter_li, grad_filter_mr, gain_blocks = deliver(bundled, norm_gain.reshape(blocks, width))
    grad_gain = gain_blocks.reshape(rows)
    return (
        grad_query,
        grad_key,
        grad_value,
        grad_key_li,
        grad_gain,
        grad_filter_mr,
        grad_filter_li,
    )


def solution(mesh):
    in_specs = (
        P("ch", "ctx"),
        P("ch", "ctx"),
        P("ch", "ctx"),
        P("ch", "ctx"),
        P("ch", "ctx"),
        P("ch"),
        P("ch", None),
        P("ch", "ctx"),
    )
    out_specs = (
        P("ch", "ctx"),
        P("ch", "ctx"),
        P("ch", "ctx"),
        P("ch", "ctx"),
        P("ch"),
        P("ch", None),
        P("ch", "ctx"),
    )
    return jax.shard_map(local, mesh=mesh, in_specs=in_specs, out_specs=out_specs, check_vma=False)
```

```python
import functools
import math

import jax
import jax.numpy as jnp
import numpy as np
from jax import lax
from jax.experimental import pallas as pl
from jax.experimental.pallas import tpu as pltpu
from jax.sharding import PartitionSpec as P

D = 8192
LANES = 128
EPSILON = 1e-06
BF16 = jnp.bfloat16
F32 = jnp.float32


def halves(table):
    high = table.astype(np.float32).astype(BF16)
    low = (table - high.astype(np.float64)).astype(np.float32).astype(BF16)
    return jnp.asarray(high), jnp.asarray(low)


def short_tables():
    place = np.arange(2 * LANES)
    angle = 2.0 * math.pi / (2 * LANES) * place[:, None] * (np.arange(LANES)[None, :] + 0.5)
    ahead = np.concatenate([np.cos(angle), -np.sin(angle)], axis=1)
    return halves(ahead) + halves(ahead.T / LANES)


def long_tables(blocks):
    radix = 2 * blocks
    total = radix * LANES
    half = np.arange(blocks) + 0.5
    outer = 2.0 * math.pi / radix * half[:, None] * np.arange(blocks)[None, :]
    first = np.concatenate([np.cos(outer), -np.sin(outer)], axis=0)
    twist = 2.0 * math.pi / total * half[:, None] * np.arange(LANES)[None, :]
    inner = 2.0 * math.pi / LANES * (np.arange(LANES)[:, None] * np.arange(LANES)[None, :] % LANES)
    cosine, sine = np.cos(inner), np.sin(inner)
    second = np.block([[cosine, -sine], [sine, cosine]])
    first_high, first_low = halves(first)
    last_high, last_low = halves(first.T * (2.0 / total))
    return (
        jnp.concatenate([first_high, first_low], axis=1),
        jnp.asarray(np.cos(twist), F32),
        jnp.asarray(np.sin(twist), F32),
        jnp.asarray(second, BF16),
        jnp.asarray(second.T, BF16),
        jnp.concatenate([last_high, last_low], axis=1),
    )


def dot(left, right):
    return jnp.dot(left, right, preferred_element_type=F32)


def split(values):
    high = values.astype(BF16)
    return high, (values - high.astype(F32)).astype(BF16)


def dot3(values, high, low):
    values_high, values_low = split(values)
    return dot(
        jnp.concatenate([values_high, values_low, values_high], axis=1),
        jnp.concatenate([high, high, low], axis=0),
    )


def dot1(values, table):
    return dot(values.astype(BF16), table)


def dot2(values, high, low):
    once = values.astype(BF16)
    return dot(jnp.concatenate([once, once], axis=1), jnp.concatenate([high, low], axis=0))


def product_kernel(key, value, product):
    product[...] = (key[...].astype(F32) * value[...].astype(F32)).astype(BF16)


def pair_kernel(cotan, filt, unread, pair):
    blocks, both = pair.shape[:2]
    pair[:, : both // 2, :] = cotan[...].reshape(blocks, -1, LANES)
    pair[:, both // 2 :, :] = filt[...].astype(BF16).reshape(blocks, -1, LANES)


def gain_column(gain):
    here = lax.broadcasted_iota(jnp.int32, (LANES, LANES), 0)
    diagonal = here == lax.broadcasted_iota(jnp.int32, (LANES, LANES), 1)
    columns = [
        jnp.sum(jnp.where(diagonal, gain[at : at + 1, :], 0.0), axis=1, keepdims=True)
        for at in range(gain.shape[0])
    ]
    return jnp.concatenate(columns, axis=0)


def mr_forward_kernel(
    key, value, prior, query, taps, unread, ahead_high, ahead_low, back_high, back_low,
    conv_out, mixed_out, window_spec, taps_spec, squares,
):
    product = key[...].astype(F32) * value[...].astype(F32)
    window = jnp.concatenate([prior[...].astype(F32), product], axis=1)
    spec = dot3(window, ahead_high[...], ahead_low[...])
    filt = dot3(taps[...], ahead_high[:LANES], ahead_low[:LANES])
    spec_re, spec_im = spec[:, :LANES], spec[:, LANES:]
    filt_re, filt_im = filt[:, :LANES], filt[:, LANES:]
    passed = jnp.concatenate(
        [spec_re * filt_re - spec_im * filt_im, spec_re * filt_im + spec_im * filt_re], axis=1
    )
    conv = dot3(passed, back_high[:, LANES:], back_low[:, LANES:])
    mixed_bf = (query[...].astype(F32) * conv).astype(BF16)
    mixed = mixed_bf.astype(F32)
    conv_out[...] = conv
    mixed_out[...] = mixed_bf
    window_spec[...] = spec
    taps_spec[...] = filt

    @pl.when(pl.program_id(0) == 0)
    def _():
        squares[...] = jnp.zeros_like(squares)

    squares[...] += jnp.sum(mixed * mixed, axis=0, keepdims=True)


def gain_block(gain, count):
    groups = count // LANES
    return gain_column(gain[pl.ds(pl.program_id(0) * groups, groups), :])


def total(parts):
    return functools.reduce(lambda left, right: left + right, [part[...] for part in parts])


def inverse_rms(squares):
    return lax.rsqrt(total(squares) / D + EPSILON)


def mr_project_kernel(grad_signal, key_li, mixed, gain, *rest):
    squares, grad_key_li, project = rest[:-2], rest[-2], rest[-1]
    grad = grad_signal[...].astype(F32)
    scaled = mixed[...].astype(F32) * inverse_rms(squares) * gain_block(gain, mixed.shape[0])
    grad_scaled = grad * scaled
    grad_key_li[...] = grad_scaled.astype(BF16)

    @pl.when(pl.program_id(0) == 0)
    def _():
        project[...] = jnp.zeros_like(project)

    project[...] += jnp.sum(grad_scaled * key_li[...].astype(F32), axis=0, keepdims=True)


def mr_backward_kernel(
    grad_signal, key_li, mixed, conv, query, gain, window_spec, taps_spec,
    ahead_high, ahead_low, back_high, back_low, *rest,
):
    count = (len(rest) - 4) // 2
    project = total(rest[:count]) / D
    grad_query, taps_and_signal, before_grad, own_grad = rest[-4:]
    inv = inverse_rms(rest[count : 2 * count])
    normed = mixed[...].astype(F32) * inv
    gain_col = gain_block(gain, mixed.shape[0])
    gate = key_li[...].astype(F32)
    signal = (normed * gain_col * gate).astype(BF16)
    grad_mixed = inv * (grad_signal[...].astype(F32) * (gate * gain_col) - normed * project)
    grad_query[...] = (grad_mixed * conv[...]).astype(BF16)
    grad_conv = grad_mixed * query[...].astype(F32)
    spec = dot2(grad_conv, ahead_high[LANES:], ahead_low[LANES:])
    spec_re, spec_im = spec[:, :LANES], spec[:, LANES:]

    def against(other):
        other_re, other_im = other[:, :LANES], other[:, LANES:]
        return jnp.concatenate(
            [spec_re * other_re + spec_im * other_im, spec_im * other_re - spec_re * other_im],
            axis=1,
        )

    taps_grad = dot1(against(window_spec[...]), back_high[:, :LANES]).astype(BF16)
    blocks, both_widths = taps_and_signal.shape[:2]
    width = both_widths // 2
    taps_and_signal[:, :width, :] = taps_grad.reshape(blocks, width, LANES)
    taps_and_signal[:, width:, :] = signal.reshape(blocks, width, LANES)
    both = dot1(against(taps_spec[...]), back_high[...])
    before_grad[...] = both[:, :LANES].astype(BF16)
    own_grad[...] = both[:, LANES:]


UNREAD = pl.BlockSpec(memory_space=pltpu.HBM)
LIMIT = pltpu.CompilerParams(vmem_limit_bytes=60 * 1024 * 1024)
PRODUCT_ROWS = 1024
PAIR_ROWS = 1024
FORWARD_ROWS = 1024
PROJECT_ROWS = 1024
BACKWARD_ROWS = 1024


def row_spec(count, width=LANES):
    return pl.BlockSpec((count, width), lambda i: (i, 0))


def whole_spec(shape):
    return pl.BlockSpec(shape, lambda i: (0,) * len(shape))


def by_rows(kernel, name, count, rows, ins, in_specs, outs, out_specs, scratch=()):
    return pl.pallas_call(
        kernel,
        grid=(rows // count,),
        in_specs=in_specs,
        out_specs=out_specs,
        out_shape=[jax.ShapeDtypeStruct(*out) for out in outs],
        scratch_shapes=scratch,
        compiler_params=LIMIT,
        name=name,
    )(*ins)


ROW = ((1, LANES), F32)


def product_of(key, value):
    rows = key.shape[0]
    each = row_spec(PRODUCT_ROWS)
    return by_rows(
        product_kernel, "product_of", PRODUCT_ROWS, rows,
        (key, value), [each] * 2, [((rows, LANES), BF16)], [each],
    )[0]


def pair_up(cotan, filt, after, blocks):
    rows = cotan.shape[0]
    width = rows // blocks
    return by_rows(
        pair_kernel, "pair_up", PAIR_ROWS, rows,
        (cotan, filt, after), [row_spec(PAIR_ROWS)] * 2 + [UNREAD],
        [((blocks, 2 * width, LANES), BF16)],
        [pl.BlockSpec((PAIR_ROWS // width, 2 * width, LANES), lambda i: (i, 0, 0))],
    )[0]


def mr_forward(key, value, prior, query, taps, after, tables):
    rows = key.shape[0]
    each, wide = row_spec(FORWARD_ROWS), row_spec(FORWARD_ROWS, 2 * LANES)
    return by_rows(
        mr_forward_kernel, "mr_forward", FORWARD_ROWS, rows,
        (key, value, prior, query, taps, after, *tables),
        [each] * 5 + [UNREAD] + [whole_spec(table.shape) for table in tables],
        [((rows, LANES), F32), ((rows, LANES), BF16)] + [((rows, 2 * LANES), F32)] * 2 + [ROW],
        [each, each, wide, wide, whole_spec((1, LANES))],
    )


def mr_project(grad_signal, key_li, mixed, gain, squares):
    rows = mixed.shape[0]
    each = row_spec(PROJECT_ROWS)
    return by_rows(
        mr_project_kernel, "mr_project", PROJECT_ROWS, rows,
        (grad_signal, key_li, mixed, gain, *squares),
        [each] * 3 + [whole_spec(gain.shape)] + [whole_spec((1, LANES))] * len(squares),
        [((rows, LANES), BF16), ROW],
        [each, whole_spec((1, LANES))],
    )


def mr_backward(
    grad_signal, key_li, mixed, conv, query, gain, window_spec, taps_spec, tables, project,
    squares, blocks,
):
    rows = mixed.shape[0]
    width = rows // blocks
    each, wide = row_spec(BACKWARD_ROWS), row_spec(BACKWARD_ROWS, 2 * LANES)
    return by_rows(
        mr_backward_kernel, "mr_backward", BACKWARD_ROWS, rows,
        (
            grad_signal, key_li, mixed, conv, query, gain, window_spec, taps_spec,
            *tables, *project, *squares,
        ),
        [each] * 5
        + [whole_spec(gain.shape)]
        + [wide] * 2
        + [whole_spec(table.shape) for table in tables]
        + [whole_spec((1, LANES))] * (len(project) + len(squares)),
        [
            ((rows, LANES), BF16), ((blocks, 2 * width, LANES), BF16), ((rows, LANES), BF16),
            ((rows, LANES), F32),
        ],
        [
            each,
            pl.BlockSpec((BACKWARD_ROWS // width, 2 * width, LANES), lambda i: (i, 0, 0)),
            each,
            each,
        ],
    )


def deliver_kernel(bundled, gain, filter_grad, taps_grad, gain_grad):
    blocks = bundled.shape[0]
    width = filter_grad.shape[0] // blocks
    values = bundled[...].astype(F32)
    filter_grad[...] = values[:, :width, :].reshape(filter_grad.shape)
    taps_grad[...] = values[:, width : 2 * width, :].reshape(taps_grad.shape)
    together = LANES // width
    step = pl.program_id(0)
    row = lax.broadcasted_iota(jnp.int32, (gain.shape[0], blocks), 0)
    block = step * blocks + lax.broadcasted_iota(jnp.int32, (gain.shape[0], blocks), 1)
    own = jnp.where((block >= row * together) & (block < (row + 1) * together), 1.0, 0.0)
    own = own.astype(BF16)
    high = values[:, 2 * width, :].astype(BF16)
    low = values[:, 2 * width + 1, :].astype(BF16)

    @pl.when(step == 0)
    def _():
        gain_grad[...] = jnp.zeros_like(gain_grad)

    gain_grad[...] += dot(own, high) + dot(own, low)

    @pl.when(step == pl.num_programs(0) - 1)
    def _():
        gain_grad[...] = gain_grad[...] / gain[...]


def deliver(bundled, gain, blocks, width):
    each = min(16, blocks)
    rows = row_spec(each * width)
    return by_rows(
        deliver_kernel, "deliver", each, blocks,
        (bundled, gain),
        [
            pl.BlockSpec((each,) + bundled.shape[1:], lambda i: (i, 0, 0)),
            whole_spec(gain.shape),
        ],
        [((blocks * width, LANES), F32)] * 2 + [(gain.shape, F32)],
        [rows, rows, whole_spec(gain.shape)],
    )


EXTRA = 8
GROUP = 8


def channel_rows(channel, blocks, width):
    return pl.ds(channel, blocks, stride=width)


def to_spectrum(flat, channels, blocks, width, offset, first, cosine, sine, second):
    pieces = [flat[channel_rows(offset + c, blocks, width), :].astype(BF16) for c in channels]
    grid = jnp.concatenate(pieces, axis=1)
    outer = dot(first[...], jnp.concatenate([grid, grid], axis=0))
    cos, sin = cosine[...], sine[...]
    turned = []
    for at in range(len(channels)):
        lanes = slice(at * LANES, (at + 1) * LANES)
        real, imag = outer[:blocks, lanes], outer[blocks:, lanes]
        turned.append(
            jnp.concatenate([real * cos + imag * sin, imag * cos - real * sin], axis=1)
        )
    return dot1(jnp.concatenate(turned, axis=0), second[...])


def from_spectrum(spec, count, blocks, second, cosine, sine, last):
    inner = dot1(spec, second[...])
    cos, sin = cosine[...], sine[...]
    turned = []
    for at in range(count):
        rows = slice(at * blocks, (at + 1) * blocks)
        real, imag = inner[rows, :LANES], inner[rows, LANES:]
        turned.append(
            jnp.concatenate([real * cos - imag * sin, imag * cos + real * sin], axis=0)
        )
    once = jnp.concatenate(turned, axis=1).astype(BF16)
    return dot(last[...], jnp.concatenate([once, once], axis=0))


def times_conj(left, right):
    left_re, left_im = left[:, :LANES], left[:, LANES:]
    right_re, right_im = right[:, :LANES], right[:, LANES:]
    return jnp.concatenate(
        [left_re * right_re + left_im * right_im, left_im * right_re - left_re * right_im], axis=1
    )


def signal_grad_kernel(
    blocks, width, pair, unread, first, cosine, sine, second, second_back, last,
    grad_out, cotan_spec, pair_flat, grad_flat,
):
    pair_flat[...] = pair[...].astype(F32)

    def one_group(step, carry):
        channels = [step * GROUP + at for at in range(GROUP)]
        rows = pl.ds(pl.multiple_of(step * (GROUP * blocks), GROUP * blocks), GROUP * blocks)

        def spectrum(offset):
            return to_spectrum(
                pair_flat, channels, blocks, 2 * width, offset, first, cosine, sine, second
            )

        moved = spectrum(0)
        cotan_spec[rows, :] = moved
        grads = from_spectrum(
            times_conj(moved, spectrum(width)), GROUP, blocks, second_back, cosine, sine, last
        )
        for at, channel in enumerate(channels):
            lanes = slice(at * LANES, (at + 1) * LANES)
            grad_flat[channel_rows(channel, blocks, width), :] = grads[:, lanes]
        return carry

    lax.fori_loop(0, width // GROUP, one_group, 0)
    grad_out[...] = grad_flat[...].astype(BF16)


def filter_grad_kernel(
    blocks, width, together, moved, cotan_spec, grad_signal, unread, first, cosine, sine, second,
    second_back, last, bundled, moved_flat, grad_flat,
):
    moved_flat[...] = moved[...].reshape(moved_flat.shape).astype(F32)
    taps = jnp.sum(moved[:, :width, :].astype(F32), axis=0).astype(BF16)
    bundled[:, width : 2 * width, :] = jnp.broadcast_to(taps[None], (blocks, width, LANES))
    terms = moved[:, width:, :].astype(F32) * grad_signal[...].astype(F32)
    sums = jnp.sum(jnp.sum(terms, axis=0), axis=1, keepdims=True)
    high = sums.astype(BF16).astype(F32)
    place = lax.broadcasted_iota(jnp.int32, (width, LANES), 0)
    place = place + lax.rem(lax.axis_index("ctx"), together) * width
    here = lax.broadcasted_iota(jnp.int32, (width, LANES), 1) == place
    lines = [jnp.sum(jnp.where(here, part, 0.0), axis=0) for part in (high, sums - high)]
    row = lax.broadcasted_iota(jnp.int32, (EXTRA, LANES), 0)
    lines = jnp.where(row == 0, lines[0][None], jnp.where(row == 1, lines[1][None], 0.0))
    bundled[:, 2 * width :, :] = jnp.broadcast_to(
        lines.astype(BF16)[None], (blocks, EXTRA, LANES)
    )

    def one_group(step, carry):
        channels = [step * GROUP + at for at in range(GROUP)]
        spec = to_spectrum(
            moved_flat, channels, blocks, 2 * width, width, first, cosine, sine, second
        )
        rows = pl.ds(pl.multiple_of(step * (GROUP * blocks), GROUP * blocks), GROUP * blocks)
        grads = from_spectrum(
            times_conj(cotan_spec[rows, :], spec), GROUP, blocks, second_back, cosine, sine, last
        )
        for at, channel in enumerate(channels):
            lanes = slice(at * LANES, (at + 1) * LANES)
            grad_flat[channel_rows(channel, blocks, width), :] = grads[:, lanes]
        return carry

    lax.fori_loop(0, width // GROUP, one_group, 0)
    bundled[:, :width, :] = grad_flat[...].reshape(blocks, width, LANES).astype(BF16)


def signal_grad(pair, after, blocks, tables):
    rows = pair.shape[0] // 2
    return by_rows(
        functools.partial(signal_grad_kernel, blocks, rows // blocks), "signal_grad", 1, 1,
        (pair, after, *tables),
        [whole_spec(pair.shape), UNREAD] + [whole_spec(table.shape) for table in tables],
        [((rows, LANES), BF16), ((rows, 2 * LANES), F32)],
        [whole_spec((rows, LANES)), whole_spec((rows, 2 * LANES))],
        [pltpu.VMEM((2 * rows, LANES), F32), pltpu.VMEM((rows, LANES), F32)],
    )


def filter_grad(moved, cotan_spec, grad_signal, after, tables):
    blocks, both, _ = moved.shape
    width = both // 2
    ins = (moved, cotan_spec, grad_signal.reshape(blocks, width, LANES))
    shape = (blocks, 2 * width + EXTRA, LANES)
    return by_rows(
        functools.partial(filter_grad_kernel, blocks, width, LANES // width), "filter_grad", 1, 1,
        (*ins, after, *tables),
        [whole_spec(value.shape) for value in ins]
        + [UNREAD]
        + [whole_spec(table.shape) for table in tables],
        [(shape, BF16)],
        [whole_spec(shape)],
        [pltpu.VMEM((2 * blocks * width, LANES), F32), pltpu.VMEM((blocks * width, LANES), F32)],
    )[0]


def swapped(rows):
    return lax.all_to_all(rows, "ctx", split_axis=0, concat_axis=0, tiled=True)


def parts_over_ch(row):
    count = lax.axis_size("ch")
    routes = [[(i, (i + step) % count) for i in range(count)] for step in range(1, count)]
    return [row] + [lax.ppermute(row, "ch", route) for route in routes]


def shifted(block, distance):
    devices = range(lax.axis_size("ctx"))
    route = [(i - distance, i) for i in devices if i - distance in devices]
    return lax.ppermute(block, "ctx", route)


def local(query_mr, key_mr, value_mr, key_li, cotangent, norm_gain, filter_mr, filter_li):
    blocks = lax.axis_size("ctx")
    rows = query_mr.shape[0]
    short = short_tables()
    long = long_tables(blocks)
    width = rows // blocks
    gain = norm_gain.reshape(-1, LANES)
    product = product_of(key_mr, value_mr)
    prior = shifted(product, 1)
    pair = pair_up(cotangent, filter_li, product, blocks)
    moved_pair = swapped(pair).reshape(2 * rows, LANES)
    grad_moved, cotan_spec = signal_grad(moved_pair, prior, blocks, long)
    grad_signal = swapped(grad_moved)
    conv, mixed, window_spec, taps_spec, squares = mr_forward(
        key_mr, value_mr, prior, query_mr, filter_mr, grad_moved, short
    )
    squares = parts_over_ch(squares)
    grad_key_li, terms = mr_project(grad_signal, key_li, mixed, gain, squares)
    grad_query, taps_and_signal, before_grad, own_grad = mr_backward(
        grad_signal, key_li, mixed, conv, query_mr, gain, window_spec, taps_spec, short,
        parts_over_ch(terms), squares, blocks,
    )
    after = shifted(before_grad, -1)
    grad_product = own_grad + after.astype(F32)
    grad_key = (grad_product * value_mr.astype(F32)).astype(BF16)
    grad_value = (grad_product * key_mr.astype(F32)).astype(BF16)
    bundled = filter_grad(swapped(taps_and_signal), cotan_spec, grad_moved, after, long)
    grad_filter_li, grad_filter_mr, gain_rows = deliver(swapped(bundled), gain, blocks, width)
    grad_gain = gain_rows.reshape(rows)
    return (
        grad_query,
        grad_key,
        grad_value,
        grad_key_li,
        grad_gain,
        grad_filter_mr,
        grad_filter_li,
    )


def solution(mesh):
    in_specs = (
        P("ch", "ctx"),
        P("ch", "ctx"),
        P("ch", "ctx"),
        P("ch", "ctx"),
        P("ch", "ctx"),
        P("ch"),
        P("ch", None),
        P("ch", "ctx"),
    )
    out_specs = (
        P("ch", "ctx"),
        P("ch", "ctx"),
        P("ch", "ctx"),
        P("ch", "ctx"),
        P("ch"),
        P("ch", None),
        P("ch", "ctx"),
    )
    return jax.shard_map(local, mesh=mesh, in_specs=in_specs, out_specs=out_specs, check_vma=False)
```

```python
import functools
import math

import jax
import jax.numpy as jnp
import numpy as np
from jax import lax
from jax.experimental import pallas as pl
from jax.experimental.pallas import tpu as pltpu
from jax.sharding import PartitionSpec as P

D = 8192
LANES = 128
EPSILON = 1e-06
BF16 = jnp.bfloat16
F32 = jnp.float32


def halves(table):
    high = table.astype(np.float32).astype(BF16)
    low = (table - high.astype(np.float64)).astype(np.float32).astype(BF16)
    return jnp.asarray(high), jnp.asarray(low)


def short_tables():
    place = np.arange(2 * LANES)
    angle = 2.0 * math.pi / (2 * LANES) * place[:, None] * (np.arange(LANES)[None, :] + 0.5)
    ahead = np.concatenate([np.cos(angle), -np.sin(angle)], axis=1)
    return halves(ahead) + halves(ahead.T / LANES)


def long_tables(blocks):
    radix = 2 * blocks
    total = radix * LANES
    half = np.arange(blocks) + 0.5
    outer = 2.0 * math.pi / radix * half[:, None] * np.arange(blocks)[None, :]
    first = np.concatenate([np.cos(outer), -np.sin(outer)], axis=0)
    twist = 2.0 * math.pi / total * half[:, None] * np.arange(LANES)[None, :]
    inner = 2.0 * math.pi / LANES * (np.arange(LANES)[:, None] * np.arange(LANES)[None, :] % LANES)
    cosine, sine = np.cos(inner), np.sin(inner)
    second = np.block([[cosine, -sine], [sine, cosine]])
    first_high, first_low = halves(first)
    last_high, last_low = halves(first.T * (2.0 / total))
    return (
        jnp.concatenate([first_high, first_low], axis=1),
        jnp.asarray(np.cos(twist), F32),
        jnp.asarray(np.sin(twist), F32),
        jnp.asarray(second, BF16),
        jnp.asarray(second.T, BF16),
        jnp.concatenate([last_high, last_low], axis=1),
    )


def dot(left, right):
    return jnp.dot(left, right, preferred_element_type=F32)


def split(values):
    high = values.astype(BF16)
    return high, (values - high.astype(F32)).astype(BF16)


def dot3(values, high, low):
    values_high, values_low = split(values)
    return dot(
        jnp.concatenate([values_high, values_low, values_high], axis=1),
        jnp.concatenate([high, high, low], axis=0),
    )


def dot1(values, table):
    return dot(values.astype(BF16), table)


def dot2(values, high, low):
    once = values.astype(BF16)
    return dot(jnp.concatenate([once, once], axis=1), jnp.concatenate([high, low], axis=0))


def product_kernel(key, value, product):
    product[...] = (key[...].astype(F32) * value[...].astype(F32)).astype(BF16)


def pair_kernel(cotan, filt, pair):
    blocks, both = pair.shape[:2]
    pair[:, : both // 2, :] = cotan[...].reshape(blocks, -1, LANES)
    pair[:, both // 2 :, :] = filt[...].astype(BF16).reshape(blocks, -1, LANES)


def gain_column(gain):
    here = lax.broadcasted_iota(jnp.int32, (LANES, LANES), 0)
    diagonal = here == lax.broadcasted_iota(jnp.int32, (LANES, LANES), 1)
    columns = [
        jnp.sum(jnp.where(diagonal, gain[at : at + 1, :], 0.0), axis=1, keepdims=True)
        for at in range(gain.shape[0])
    ]
    return jnp.concatenate(columns, axis=0)


def mr_forward_kernel(
    key, value, prior, query, taps, ahead_high, ahead_low, back_high, back_low,
    conv_out, mixed_out, window_spec, taps_spec, squares,
):
    product = key[...].astype(F32) * value[...].astype(F32)
    window = jnp.concatenate([prior[...].astype(F32), product], axis=1)
    spec = dot3(window, ahead_high[...], ahead_low[...])
    filt = dot3(taps[...], ahead_high[:LANES], ahead_low[:LANES])
    spec_re, spec_im = spec[:, :LANES], spec[:, LANES:]
    filt_re, filt_im = filt[:, :LANES], filt[:, LANES:]
    passed = jnp.concatenate(
        [spec_re * filt_re - spec_im * filt_im, spec_re * filt_im + spec_im * filt_re], axis=1
    )
    conv = dot3(passed, back_high[:, LANES:], back_low[:, LANES:])
    mixed_bf = (query[...].astype(F32) * conv).astype(BF16)
    mixed = mixed_bf.astype(F32)
    conv_out[...] = conv
    mixed_out[...] = mixed_bf
    window_spec[...] = spec
    taps_spec[...] = filt

    @pl.when(pl.program_id(0) == 0)
    def _():
        squares[...] = jnp.zeros_like(squares)

    squares[...] += jnp.sum(mixed * mixed, axis=0, keepdims=True)


def gain_block(gain, count):
    groups = count // LANES
    return gain_column(gain[pl.ds(pl.program_id(0) * groups, groups), :])


def total(parts):
    return functools.reduce(lambda left, right: left + right, [part[...] for part in parts])


def inverse_rms(squares):
    return lax.rsqrt(total(squares) / D + EPSILON)


def gate_kernel(mixed, key_li, gain, *rest):
    squares, signal, inv_out = rest[:-2], rest[-2], rest[-1]
    inv = inverse_rms(squares)
    inv_out[...] = inv
    scaled = mixed[...].astype(F32) * inv * gain_block(gain, mixed.shape[0])
    signal[...] = (scaled * key_li[...].astype(F32)).astype(BF16)


def mr_project_kernel(grad_signal, key_li, mixed, gain, inv_rms, grad_key_li, project):
    grad = grad_signal[...].reshape(mixed.shape).astype(F32)
    scaled = mixed[...].astype(F32) * inv_rms[...] * gain_block(gain, mixed.shape[0])
    grad_scaled = grad * scaled
    grad_key_li[...] = grad_scaled.astype(BF16)

    @pl.when(pl.program_id(0) == 0)
    def _():
        project[...] = jnp.zeros_like(project)

    project[...] += jnp.sum(grad_scaled * key_li[...].astype(F32), axis=0, keepdims=True)


def mr_backward_kernel(
    grad_signal, key_li, mixed, conv, query, gain, inv_rms, window_spec, taps_spec,
    ahead_high, ahead_low, back_high, back_low, *rest,
):
    project = total(rest[:-4]) / D
    grad_query, taps_grad, before_grad, own_grad = rest[-4:]
    inv = inv_rms[...]
    normed = mixed[...].astype(F32) * inv
    gated = key_li[...].astype(F32) * gain_block(gain, mixed.shape[0])
    grad = grad_signal[...].reshape(mixed.shape).astype(F32)
    grad_mixed = inv * (grad * gated - normed * project)
    grad_query[...] = (grad_mixed * conv[...]).astype(BF16)
    grad_conv = grad_mixed * query[...].astype(F32)
    spec = dot2(grad_conv, ahead_high[LANES:], ahead_low[LANES:])
    spec_re, spec_im = spec[:, :LANES], spec[:, LANES:]

    def against(other):
        other_re, other_im = other[:, :LANES], other[:, LANES:]
        return jnp.concatenate(
            [spec_re * other_re + spec_im * other_im, spec_im * other_re - spec_re * other_im],
            axis=1,
        )

    taps_grad[...] = dot1(against(window_spec[...]), back_high[:, :LANES]).astype(BF16)
    both = dot1(against(taps_spec[...]), back_high[...])
    before_grad[...] = both[:, :LANES].astype(BF16)
    own_grad[...] = both[:, LANES:]


UNREAD = pl.BlockSpec(memory_space=pltpu.HBM)
LIMIT = pltpu.CompilerParams(vmem_limit_bytes=60 * 1024 * 1024)
PRODUCT_ROWS = 1024
PAIR_ROWS = 1024
FORWARD_ROWS = 1024
GATE_ROWS = 1024
PROJECT_ROWS = 1024
BACKWARD_ROWS = 1024


def row_spec(count, width=LANES):
    return pl.BlockSpec((count, width), lambda i: (i, 0))


def whole_spec(shape):
    return pl.BlockSpec(shape, lambda i: (0,) * len(shape))


def by_rows(kernel, name, count, rows, ins, in_specs, outs, out_specs, scratch=()):
    return pl.pallas_call(
        kernel,
        grid=(rows // count,),
        in_specs=in_specs,
        out_specs=out_specs,
        out_shape=[jax.ShapeDtypeStruct(*out) for out in outs],
        scratch_shapes=scratch,
        compiler_params=LIMIT,
        name=name,
    )(*ins)


ROW = ((1, LANES), F32)


def product_of(key, value):
    rows = key.shape[0]
    each = row_spec(PRODUCT_ROWS)
    return by_rows(
        product_kernel, "product_of", PRODUCT_ROWS, rows,
        (key, value), [each] * 2, [((rows, LANES), BF16)], [each],
    )[0]


def pair_up(cotan, filt, blocks):
    rows = cotan.shape[0]
    width = rows // blocks
    return by_rows(
        pair_kernel, "pair_up", PAIR_ROWS, rows,
        (cotan, filt), [row_spec(PAIR_ROWS)] * 2,
        [((blocks, 2 * width, LANES), BF16)],
        [pl.BlockSpec((PAIR_ROWS // width, 2 * width, LANES), lambda i: (i, 0, 0))],
    )[0]


def mr_forward(key, value, prior, query, taps, tables):
    rows = key.shape[0]
    each, wide = row_spec(FORWARD_ROWS), row_spec(FORWARD_ROWS, 2 * LANES)
    return by_rows(
        mr_forward_kernel, "mr_forward", FORWARD_ROWS, rows,
        (key, value, prior, query, taps, *tables),
        [each] * 5 + [whole_spec(table.shape) for table in tables],
        [((rows, LANES), F32), ((rows, LANES), BF16)] + [((rows, 2 * LANES), F32)] * 2 + [ROW],
        [each, each, wide, wide, whole_spec((1, LANES))],
    )


def gate(mixed, key_li, gain, squares):
    rows = mixed.shape[0]
    each = row_spec(GATE_ROWS)
    return by_rows(
        gate_kernel, "gate", GATE_ROWS, rows,
        (mixed, key_li, gain, *squares),
        [each] * 2 + [whole_spec(gain.shape)] + [whole_spec((1, LANES))] * len(squares),
        [((rows, LANES), BF16), ROW],
        [each, whole_spec((1, LANES))],
    )


def first_half_spec(pair, count):
    width = pair.shape[1] // 2
    return pl.BlockSpec((count // width, width, LANES), lambda i: (i, 0, 0))


def mr_project(moved, key_li, mixed, gain, inv_rms):
    rows = mixed.shape[0]
    each = row_spec(PROJECT_ROWS)
    return by_rows(
        mr_project_kernel, "mr_project", PROJECT_ROWS, rows,
        (moved, key_li, mixed, gain, inv_rms),
        [first_half_spec(moved, PROJECT_ROWS)]
        + [each] * 2
        + [whole_spec(gain.shape), whole_spec((1, LANES))],
        [((rows, LANES), BF16), ROW],
        [each, whole_spec((1, LANES))],
    )


def mr_backward(
    moved, key_li, mixed, conv, query, gain, inv_rms, window_spec, taps_spec, tables, project
):
    rows = mixed.shape[0]
    each, wide = row_spec(BACKWARD_ROWS), row_spec(BACKWARD_ROWS, 2 * LANES)
    return by_rows(
        mr_backward_kernel, "mr_backward", BACKWARD_ROWS, rows,
        (
            moved, key_li, mixed, conv, query, gain, inv_rms, window_spec, taps_spec,
            *tables, *project,
        ),
        [first_half_spec(moved, BACKWARD_ROWS)]
        + [each] * 4
        + [whole_spec(gain.shape), whole_spec((1, LANES))]
        + [wide] * 2
        + [whole_spec(table.shape) for table in tables]
        + [whole_spec((1, LANES))] * len(project),
        [((rows, LANES), BF16)] * 3 + [((rows, LANES), F32)],
        [each] * 4,
    )


def hold(values, after):
    return pl.pallas_call(
        lambda *refs: None,
        in_specs=[UNREAD] * 2,
        out_specs=UNREAD,
        out_shape=jax.ShapeDtypeStruct(values.shape, values.dtype),
        input_output_aliases={0: 0},
        name="hold",
    )(values, after)


def bundle_kernel(bundled, taps_grad, unread, out):
    taps = jnp.sum(taps_grad[...].astype(F32), axis=0).astype(BF16)
    out[...] = jnp.broadcast_to(taps[None], out.shape)


def bundle(bundled, taps_grad, after):
    whole = taps_grad.shape
    return pl.pallas_call(
        bundle_kernel,
        grid=(1,),
        in_specs=[UNREAD, whole_spec(whole), UNREAD],
        out_specs=pl.BlockSpec(whole, lambda i: (0, 1, 0)),
        out_shape=jax.ShapeDtypeStruct(bundled.shape, bundled.dtype),
        input_output_aliases={0: 0},
        compiler_params=LIMIT,
        name="bundle",
    )(bundled, taps_grad, after)


def deliver_kernel(bundled, gain, filter_grad, taps_grad, gain_grad):
    blocks = bundled.shape[0]
    width = filter_grad.shape[0] // blocks
    values = bundled[...].astype(F32)
    filter_grad[...] = values[:, :width, :].reshape(filter_grad.shape)
    taps_grad[...] = values[:, width : 2 * width, :].reshape(taps_grad.shape)
    together = LANES // width
    step = pl.program_id(0)
    row = lax.broadcasted_iota(jnp.int32, (gain.shape[0], blocks), 0)
    block = step * blocks + lax.broadcasted_iota(jnp.int32, (gain.shape[0], blocks), 1)
    own = jnp.where((block >= row * together) & (block < (row + 1) * together), 1.0, 0.0)
    own = own.astype(BF16)
    high = values[:, 2 * width, :].astype(BF16)
    low = values[:, 2 * width + 1, :].astype(BF16)

    @pl.when(step == 0)
    def _():
        gain_grad[...] = jnp.zeros_like(gain_grad)

    gain_grad[...] += dot(own, high) + dot(own, low)

    @pl.when(step == pl.num_programs(0) - 1)
    def _():
        gain_grad[...] = gain_grad[...] / gain[...]


def deliver(bundled, gain, blocks, width):
    each = min(32, blocks)
    rows = row_spec(each * width)
    return by_rows(
        deliver_kernel, "deliver", each, blocks,
        (bundled, gain),
        [
            pl.BlockSpec((each,) + bundled.shape[1:], lambda i: (i, 0, 0)),
            whole_spec(gain.shape),
        ],
        [((blocks * width, LANES), F32)] * 2 + [(gain.shape, F32)],
        [rows, rows, whole_spec(gain.shape)],
    )


EXTRA = 8
GROUP = 16


def channel_rows(channel, blocks, width):
    return pl.ds(channel, blocks, stride=width)


def to_spectrum(flat, channels, blocks, width, offset, first, cosine, sine, second):
    pieces = [flat[channel_rows(offset + c, blocks, width), :].astype(BF16) for c in channels]
    grid = jnp.concatenate(pieces, axis=1)
    outer = dot(first[...], jnp.concatenate([grid, grid], axis=0))
    cos, sin = cosine[...], sine[...]
    turned = []
    for at in range(len(channels)):
        lanes = slice(at * LANES, (at + 1) * LANES)
        real, imag = outer[:blocks, lanes], outer[blocks:, lanes]
        turned.append(
            jnp.concatenate([real * cos + imag * sin, imag * cos - real * sin], axis=1)
        )
    return dot1(jnp.concatenate(turned, axis=0), second[...])


def from_spectrum(spec, count, blocks, second, cosine, sine, last):
    inner = dot1(spec, second[...])
    cos, sin = cosine[...], sine[...]
    turned = []
    for at in range(count):
        rows = slice(at * blocks, (at + 1) * blocks)
        real, imag = inner[rows, :LANES], inner[rows, LANES:]
        turned.append(
            jnp.concatenate([real * cos - imag * sin, imag * cos + real * sin], axis=0)
        )
    once = jnp.concatenate(turned, axis=1).astype(BF16)
    return dot(last[...], jnp.concatenate([once, once], axis=0))


def times_conj(left, right):
    left_re, left_im = left[:, :LANES], left[:, LANES:]
    right_re, right_im = right[:, :LANES], right[:, LANES:]
    return jnp.concatenate(
        [left_re * right_re + left_im * right_im, left_im * right_re - left_re * right_im], axis=1
    )


def signal_grad_kernel(
    blocks, width, pair, signal, first, cosine, sine, second, second_back, last,
    outward, cotan_spec, pair_flat, grad_flat,
):
    outward[:, width:, :] = signal[...].reshape(blocks, width, LANES)
    pair_flat[...] = pair[...].astype(F32)

    def one_group(step, carry):
        channels = [step * GROUP + at for at in range(GROUP)]
        rows = pl.ds(pl.multiple_of(step * (GROUP * blocks), GROUP * blocks), GROUP * blocks)

        def spectrum(offset):
            return to_spectrum(
                pair_flat, channels, blocks, 2 * width, offset, first, cosine, sine, second
            )

        moved = spectrum(0)
        cotan_spec[rows, :] = moved
        grads = from_spectrum(
            times_conj(moved, spectrum(width)), GROUP, blocks, second_back, cosine, sine, last
        )
        for at, channel in enumerate(channels):
            lanes = slice(at * LANES, (at + 1) * LANES)
            grad_flat[channel_rows(channel, blocks, width), :] = grads[:, lanes]
        return carry

    lax.fori_loop(0, width // GROUP, one_group, 0)
    outward[:, :width, :] = grad_flat[...].astype(BF16).reshape(blocks, width, LANES)


def filter_grad_kernel(
    blocks, width, together, signal, cotan_spec, grad_signal, unread, first, cosine, sine, second,
    second_back, last, bundled, signal_flat, grad_flat,
):
    values = signal[...].astype(F32)
    signal_flat[...] = values.reshape(signal_flat.shape)
    terms = values * grad_signal[...].astype(F32)
    sums = jnp.sum(jnp.sum(terms, axis=0), axis=1, keepdims=True)
    high = sums.astype(BF16).astype(F32)
    place = lax.broadcasted_iota(jnp.int32, (width, LANES), 0)
    place = place + lax.rem(lax.axis_index("ctx"), together) * width
    here = lax.broadcasted_iota(jnp.int32, (width, LANES), 1) == place
    lines = [jnp.sum(jnp.where(here, part, 0.0), axis=0) for part in (high, sums - high)]
    row = lax.broadcasted_iota(jnp.int32, (EXTRA, LANES), 0)
    lines = jnp.where(row == 0, lines[0][None], jnp.where(row == 1, lines[1][None], 0.0))
    bundled[:, 2 * width :, :] = jnp.broadcast_to(
        lines.astype(BF16)[None], (blocks, EXTRA, LANES)
    )

    def one_group(step, carry):
        channels = [step * GROUP + at for at in range(GROUP)]
        spec = to_spectrum(
            signal_flat, channels, blocks, width, 0, first, cosine, sine, second
        )
        rows = pl.ds(pl.multiple_of(step * (GROUP * blocks), GROUP * blocks), GROUP * blocks)
        grads = from_spectrum(
            times_conj(cotan_spec[rows, :], spec), GROUP, blocks, second_back, cosine, sine, last
        )
        for at, channel in enumerate(channels):
            lanes = slice(at * LANES, (at + 1) * LANES)
            grad_flat[channel_rows(channel, blocks, width), :] = grads[:, lanes]
        return carry

    lax.fori_loop(0, width // GROUP, one_group, 0)
    bundled[:, :width, :] = grad_flat[...].reshape(blocks, width, LANES).astype(BF16)


def signal_grad(pair, signal, blocks, tables):
    rows = pair.shape[0] // 2
    width = rows // blocks
    shape = (blocks, 2 * width, LANES)
    ins = (pair, signal, *tables)
    return by_rows(
        functools.partial(signal_grad_kernel, blocks, width), "signal_grad", 1, 1,
        ins, [whole_spec(value.shape) for value in ins],
        [(shape, BF16), ((rows, 2 * LANES), F32)],
        [whole_spec(shape), whole_spec((rows, 2 * LANES))],
        [pltpu.VMEM((2 * rows, LANES), F32), pltpu.VMEM((rows, LANES), F32)],
    )


def filter_grad(moved, cotan_spec, outward, after, tables):
    blocks, both, _ = moved.shape
    width = both // 2
    half = (blocks, width, LANES)
    shape = (blocks, 2 * width + EXTRA, LANES)
    return by_rows(
        functools.partial(filter_grad_kernel, blocks, width, LANES // width), "filter_grad", 1, 1,
        (moved, cotan_spec, outward, after, *tables),
        [
            pl.BlockSpec(half, lambda i: (0, 1, 0)),
            whole_spec(cotan_spec.shape),
            whole_spec(half),
            UNREAD,
        ]
        + [whole_spec(table.shape) for table in tables],
        [(shape, BF16)],
        [whole_spec(shape)],
        [pltpu.VMEM((blocks * width, LANES), F32)] * 2,
    )[0]


def swapped(rows):
    return lax.all_to_all(rows, "ctx", split_axis=0, concat_axis=0, tiled=True)


def parts_over_ch(row):
    count = lax.axis_size("ch")
    routes = [[(i, (i + step) % count) for i in range(count)] for step in range(1, count)]
    return [row] + [lax.ppermute(row, "ch", route) for route in routes]


def shifted(block, distance):
    devices = range(lax.axis_size("ctx"))
    route = [(i - distance, i) for i in devices if i - distance in devices]
    return lax.ppermute(block, "ctx", route)


def local(query_mr, key_mr, value_mr, key_li, cotangent, norm_gain, filter_mr, filter_li):
    blocks = lax.axis_size("ctx")
    rows = query_mr.shape[0]
    short = short_tables()
    long = long_tables(blocks)
    width = rows // blocks
    gain = norm_gain.reshape(-1, LANES)
    prior = shifted(product_of(key_mr, value_mr), 1)
    pair = hold(pair_up(cotangent, filter_li, blocks), prior)
    moved_pair = swapped(pair).reshape(2 * rows, LANES)
    conv, mixed, window_spec, taps_spec, squares = mr_forward(
        key_mr, value_mr, prior, query_mr, filter_mr, short
    )
    signal, inv_rms = gate(mixed, key_li, gain, parts_over_ch(squares))
    outward, cotan_spec = signal_grad(moved_pair, signal, blocks, long)
    moved = swapped(outward)
    grad_key_li, terms = mr_project(moved, key_li, mixed, gain, inv_rms)
    grad_query, taps_grad, before_grad, own_grad = mr_backward(
        moved, key_li, mixed, conv, query_mr, gain, inv_rms, window_spec, taps_spec, short,
        parts_over_ch(terms),
    )
    after = shifted(before_grad, -1)
    grad_product = own_grad + after.astype(F32)
    grad_key = (grad_product * value_mr.astype(F32)).astype(BF16)
    grad_value = (grad_product * key_mr.astype(F32)).astype(BF16)
    moved_taps = swapped(taps_grad).reshape(blocks, width, LANES)
    bundled = bundle(
        filter_grad(moved, cotan_spec, outward, taps_grad, long), moved_taps, after
    )
    grad_filter_li, grad_filter_mr, gain_rows = deliver(swapped(bundled), gain, blocks, width)
    grad_gain = gain_rows.reshape(rows)
    return (
        grad_query,
        grad_key,
        grad_value,
        grad_key_li,
        grad_gain,
        grad_filter_mr,
        grad_filter_li,
    )


def solution(mesh):
    in_specs = (
        P("ch", "ctx"),
        P("ch", "ctx"),
        P("ch", "ctx"),
        P("ch", "ctx"),
        P("ch", "ctx"),
        P("ch"),
        P("ch", None),
        P("ch", "ctx"),
    )
    out_specs = (
        P("ch", "ctx"),
        P("ch", "ctx"),
        P("ch", "ctx"),
        P("ch", "ctx"),
        P("ch"),
        P("ch", None),
        P("ch", "ctx"),
    )
    return jax.shard_map(local, mesh=mesh, in_specs=in_specs, out_specs=out_specs, check_vma=False)
```

```python
import functools
import math

import jax
import jax.numpy as jnp
import numpy as np
from jax import lax
from jax.experimental import pallas as pl
from jax.experimental.pallas import tpu as pltpu
from jax.sharding import PartitionSpec as P

D = 8192
LANES = 128
EPSILON = 1e-06
BF16 = jnp.bfloat16
F32 = jnp.float32


def halves(table):
    high = table.astype(np.float32).astype(BF16)
    low = (table - high.astype(np.float64)).astype(np.float32).astype(BF16)
    return jnp.asarray(high), jnp.asarray(low)


def short_tables():
    place = np.arange(2 * LANES)
    angle = 2.0 * math.pi / (2 * LANES) * place[:, None] * (np.arange(LANES)[None, :] + 0.5)
    ahead = np.concatenate([np.cos(angle), -np.sin(angle)], axis=1)
    return halves(ahead) + halves(ahead.T / LANES)


def long_tables(blocks):
    radix = 2 * blocks
    total = radix * LANES
    half = np.arange(blocks) + 0.5
    outer = 2.0 * math.pi / radix * half[:, None] * np.arange(blocks)[None, :]
    first = np.concatenate([np.cos(outer), -np.sin(outer)], axis=0)
    twist = 2.0 * math.pi / total * half[:, None] * np.arange(LANES)[None, :]
    inner = 2.0 * math.pi / LANES * (np.arange(LANES)[:, None] * np.arange(LANES)[None, :] % LANES)
    cosine, sine = np.cos(inner), np.sin(inner)
    second = np.block([[cosine, -sine], [sine, cosine]])
    first_high, first_low = halves(first)
    last_high, last_low = halves(first.T * (2.0 / total))
    return (
        jnp.concatenate([first_high, first_low], axis=1),
        jnp.asarray(np.cos(twist), F32),
        jnp.asarray(np.sin(twist), F32),
        jnp.asarray(second, BF16),
        jnp.asarray(second.T, BF16),
        jnp.concatenate([last_high, last_low], axis=1),
    )


def dot(left, right):
    return jnp.dot(left, right, preferred_element_type=F32)


def split(values):
    high = values.astype(BF16)
    return high, (values - high.astype(F32)).astype(BF16)


def dot3(values, high, low):
    values_high, values_low = split(values)
    return dot(
        jnp.concatenate([values_high, values_low, values_high], axis=1),
        jnp.concatenate([high, high, low], axis=0),
    )


def dot1(values, table):
    return dot(values.astype(BF16), table)


def dot2(values, high, low):
    once = values.astype(BF16)
    return dot(jnp.concatenate([once, once], axis=1), jnp.concatenate([high, low], axis=0))


def product_kernel(key, value, product):
    product[...] = (key[...].astype(F32) * value[...].astype(F32)).astype(BF16)


def pair_kernel(cotan, filt, pair):
    blocks, both = pair.shape[:2]
    pair[:, : both // 2, :] = cotan[...].reshape(blocks, -1, LANES)
    pair[:, both // 2 :, :] = filt[...].astype(BF16).reshape(blocks, -1, LANES)


def gain_column(gain):
    here = lax.broadcasted_iota(jnp.int32, (LANES, LANES), 0)
    diagonal = here == lax.broadcasted_iota(jnp.int32, (LANES, LANES), 1)
    columns = [
        jnp.sum(jnp.where(diagonal, gain[at : at + 1, :], 0.0), axis=1, keepdims=True)
        for at in range(gain.shape[0])
    ]
    return jnp.concatenate(columns, axis=0)


def mr_forward_kernel(
    key, value, prior, query, taps, unread, ahead_high, ahead_low, back_high, back_low,
    conv_out, mixed_out, window_spec, taps_spec, squares,
):
    product = key[...].astype(F32) * value[...].astype(F32)
    window = jnp.concatenate([prior[...].astype(F32), product], axis=1)
    spec = dot3(window, ahead_high[...], ahead_low[...])
    filt = dot3(taps[...], ahead_high[:LANES], ahead_low[:LANES])
    spec_re, spec_im = spec[:, :LANES], spec[:, LANES:]
    filt_re, filt_im = filt[:, :LANES], filt[:, LANES:]
    passed = jnp.concatenate(
        [spec_re * filt_re - spec_im * filt_im, spec_re * filt_im + spec_im * filt_re], axis=1
    )
    conv = dot3(passed, back_high[:, LANES:], back_low[:, LANES:])
    mixed_bf = (query[...].astype(F32) * conv).astype(BF16)
    mixed = mixed_bf.astype(F32)
    conv_out[...] = conv
    mixed_out[...] = mixed_bf
    window_spec[...] = spec
    taps_spec[...] = filt

    @pl.when(pl.program_id(0) == 0)
    def _():
        squares[...] = jnp.zeros_like(squares)

    squares[...] += jnp.sum(mixed * mixed, axis=0, keepdims=True)


def gain_block(gain, count):
    groups = count // LANES
    return gain_column(gain[pl.ds(pl.program_id(0) * groups, groups), :])


def total(parts):
    return functools.reduce(lambda left, right: left + right, [part[...] for part in parts])


def inverse_rms(squares):
    return lax.rsqrt(total(squares) / D + EPSILON)


def mr_project_kernel(grad_signal, key_li, mixed, gain, *rest):
    squares, grad_key_li, project = rest[:-2], rest[-2], rest[-1]
    grad = grad_signal[...].astype(F32)
    scaled = mixed[...].astype(F32) * inverse_rms(squares) * gain_block(gain, mixed.shape[0])
    grad_scaled = grad * scaled
    grad_key_li[...] = grad_scaled.astype(BF16)

    @pl.when(pl.program_id(0) == 0)
    def _():
        project[...] = jnp.zeros_like(project)

    project[...] += jnp.sum(grad_scaled * key_li[...].astype(F32), axis=0, keepdims=True)


def against(spec, other):
    spec_re, spec_im = spec[:, :LANES], spec[:, LANES:]
    other_re, other_im = other[:, :LANES], other[:, LANES:]
    return jnp.concatenate(
        [spec_re * other_re + spec_im * other_im, spec_im * other_re - spec_re * other_im], axis=1
    )


def mixed_gradient(grad_signal, key_li, mixed, gain, project, squares):
    inv = inverse_rms(squares)
    normed = mixed[...].astype(F32) * inv
    gated = key_li[...].astype(F32) * gain_block(gain, mixed.shape[0])
    grads = grad_signal[...].astype(F32) * gated - normed * (total(project) / D)
    return inv * grads, normed * gated


def taps_grad_kernel(
    grad_signal, key_li, mixed, query, gain, window_spec,
    ahead_high, ahead_low, back_high, *rest,
):
    count = (len(rest) - 2) // 2
    taps_and_signal, spec_out = rest[-2:]
    grad_mixed, signal = mixed_gradient(
        grad_signal, key_li, mixed, gain, rest[:count], rest[count : 2 * count]
    )
    spec = dot2(
        grad_mixed * query[...].astype(F32), ahead_high[LANES:], ahead_low[LANES:]
    )
    spec_out[...] = spec
    taps_grad = dot1(against(spec, window_spec[...]), back_high[:, :LANES]).astype(BF16)
    blocks, both_widths = taps_and_signal.shape[:2]
    width = both_widths // 2
    taps_and_signal[:, :width, :] = taps_grad.reshape(blocks, width, LANES)
    taps_and_signal[:, width:, :] = signal.astype(BF16).reshape(blocks, width, LANES)


def product_grad_kernel(
    grad_signal, key_li, mixed, conv, gain, spec, taps_spec, back_high, *rest
):
    count = (len(rest) - 3) // 2
    grad_query, before_grad, own_grad = rest[-3:]
    grad_mixed, _ = mixed_gradient(
        grad_signal, key_li, mixed, gain, rest[:count], rest[count : 2 * count]
    )
    grad_query[...] = (grad_mixed * conv[...]).astype(BF16)
    both = dot1(against(spec[...], taps_spec[...]), back_high[...])
    before_grad[...] = both[:, :LANES].astype(BF16)
    own_grad[...] = both[:, LANES:]


UNREAD = pl.BlockSpec(memory_space=pltpu.HBM)
LIMIT = pltpu.CompilerParams(vmem_limit_bytes=60 * 1024 * 1024)
PRODUCT_ROWS = 1024
PAIR_ROWS = 1024
FORWARD_ROWS = 1024
PROJECT_ROWS = 1024
BACKWARD_ROWS = 1024


def row_spec(count, width=LANES):
    return pl.BlockSpec((count, width), lambda i: (i, 0))


def whole_spec(shape):
    return pl.BlockSpec(shape, lambda i: (0,) * len(shape))


def by_rows(kernel, name, count, rows, ins, in_specs, outs, out_specs, scratch=()):
    return pl.pallas_call(
        kernel,
        grid=(rows // count,),
        in_specs=in_specs,
        out_specs=out_specs,
        out_shape=[jax.ShapeDtypeStruct(*out) for out in outs],
        scratch_shapes=scratch,
        compiler_params=LIMIT,
        name=name,
    )(*ins)


ROW = ((1, LANES), F32)


def product_of(key, value):
    rows = key.shape[0]
    each = row_spec(PRODUCT_ROWS)
    return by_rows(
        product_kernel, "product_of", PRODUCT_ROWS, rows,
        (key, value), [each] * 2, [((rows, LANES), BF16)], [each],
    )[0]


def pair_up(cotan, filt, blocks):
    rows = cotan.shape[0]
    width = rows // blocks
    return by_rows(
        pair_kernel, "pair_up", PAIR_ROWS, rows,
        (cotan, filt), [row_spec(PAIR_ROWS)] * 2,
        [((blocks, 2 * width, LANES), BF16)],
        [pl.BlockSpec((PAIR_ROWS // width, 2 * width, LANES), lambda i: (i, 0, 0))],
    )[0]


def mr_forward(key, value, prior, query, taps, after, tables):
    rows = key.shape[0]
    each, wide = row_spec(FORWARD_ROWS), row_spec(FORWARD_ROWS, 2 * LANES)
    return by_rows(
        mr_forward_kernel, "mr_forward", FORWARD_ROWS, rows,
        (key, value, prior, query, taps, after, *tables),
        [each] * 5 + [UNREAD] + [whole_spec(table.shape) for table in tables],
        [((rows, LANES), F32), ((rows, LANES), BF16)] + [((rows, 2 * LANES), F32)] * 2 + [ROW],
        [each, each, wide, wide, whole_spec((1, LANES))],
    )


def mr_project(grad_signal, key_li, mixed, gain, squares):
    rows = mixed.shape[0]
    each = row_spec(PROJECT_ROWS)
    return by_rows(
        mr_project_kernel, "mr_project", PROJECT_ROWS, rows,
        (grad_signal, key_li, mixed, gain, *squares),
        [each] * 3 + [whole_spec(gain.shape)] + [whole_spec((1, LANES))] * len(squares),
        [((rows, LANES), BF16), ROW],
        [each, whole_spec((1, LANES))],
    )


def taps_grad_of(
    grad_signal, key_li, mixed, query, gain, window_spec, tables, project, squares, blocks
):
    rows = mixed.shape[0]
    width = rows // blocks
    each, wide = row_spec(BACKWARD_ROWS), row_spec(BACKWARD_ROWS, 2 * LANES)
    return by_rows(
        taps_grad_kernel, "taps_grad_of", BACKWARD_ROWS, rows,
        (grad_signal, key_li, mixed, query, gain, window_spec, *tables[:3], *project, *squares),
        [each] * 4
        + [whole_spec(gain.shape), wide]
        + [whole_spec(table.shape) for table in tables[:3]]
        + [whole_spec((1, LANES))] * (len(project) + len(squares)),
        [((blocks, 2 * width, LANES), BF16), ((rows, 2 * LANES), F32)],
        [pl.BlockSpec((BACKWARD_ROWS // width, 2 * width, LANES), lambda i: (i, 0, 0)), wide],
    )


def product_grad_of(
    grad_signal, key_li, mixed, conv, gain, spec, taps_spec, tables, project, squares
):
    rows = mixed.shape[0]
    each, wide = row_spec(BACKWARD_ROWS), row_spec(BACKWARD_ROWS, 2 * LANES)
    return by_rows(
        product_grad_kernel, "product_grad_of", BACKWARD_ROWS, rows,
        (
            grad_signal, key_li, mixed, conv, gain, spec, taps_spec, tables[2],
            *project, *squares,
        ),
        [each] * 4
        + [whole_spec(gain.shape), wide, wide, whole_spec(tables[2].shape)]
        + [whole_spec((1, LANES))] * (len(project) + len(squares)),
        [((rows, LANES), BF16)] * 2 + [((rows, LANES), F32)],
        [each] * 3,
    )


def deliver_kernel(bundled, gain, filter_grad, taps_grad, gain_grad):
    blocks = bundled.shape[0]
    width = filter_grad.shape[0] // blocks
    values = bundled[...].astype(F32)
    filter_grad[...] = values[:, :width, :].reshape(filter_grad.shape)
    taps_grad[...] = values[:, width : 2 * width, :].reshape(taps_grad.shape)
    together = LANES // width
    step = pl.program_id(0)
    row = lax.broadcasted_iota(jnp.int32, (gain.shape[0], blocks), 0)
    block = step * blocks + lax.broadcasted_iota(jnp.int32, (gain.shape[0], blocks), 1)
    own = jnp.where((block >= row * together) & (block < (row + 1) * together), 1.0, 0.0)
    own = own.astype(BF16)
    high = values[:, 2 * width, :].astype(BF16)
    low = values[:, 2 * width + 1, :].astype(BF16)

    @pl.when(step == 0)
    def _():
        gain_grad[...] = jnp.zeros_like(gain_grad)

    gain_grad[...] += dot(own, high) + dot(own, low)

    @pl.when(step == pl.num_programs(0) - 1)
    def _():
        gain_grad[...] = gain_grad[...] / gain[...]


def deliver(bundled, gain, blocks, width):
    each = min(32, blocks)
    rows = row_spec(each * width)
    return by_rows(
        deliver_kernel, "deliver", each, blocks,
        (bundled, gain),
        [
            pl.BlockSpec((each,) + bundled.shape[1:], lambda i: (i, 0, 0)),
            whole_spec(gain.shape),
        ],
        [((blocks * width, LANES), F32)] * 2 + [(gain.shape, F32)],
        [rows, rows, whole_spec(gain.shape)],
    )


EXTRA = 8
GROUP = 16


def channel_rows(channel, blocks, width):
    return pl.ds(channel, blocks, stride=width)


def to_spectrum(flat, channels, blocks, width, offset, first, cosine, sine, second):
    pieces = [flat[channel_rows(offset + c, blocks, width), :].astype(BF16) for c in channels]
    grid = jnp.concatenate(pieces, axis=1)
    outer = dot(first[...], jnp.concatenate([grid, grid], axis=0))
    cos, sin = cosine[...], sine[...]
    turned = []
    for at in range(len(channels)):
        lanes = slice(at * LANES, (at + 1) * LANES)
        real, imag = outer[:blocks, lanes], outer[blocks:, lanes]
        turned.append(
            jnp.concatenate([real * cos + imag * sin, imag * cos - real * sin], axis=1)
        )
    return dot1(jnp.concatenate(turned, axis=0), second[...])


def from_spectrum(spec, count, blocks, second, cosine, sine, last):
    inner = dot1(spec, second[...])
    cos, sin = cosine[...], sine[...]
    turned = []
    for at in range(count):
        rows = slice(at * blocks, (at + 1) * blocks)
        real, imag = inner[rows, :LANES], inner[rows, LANES:]
        turned.append(
            jnp.concatenate([real * cos - imag * sin, imag * cos + real * sin], axis=0)
        )
    once = jnp.concatenate(turned, axis=1).astype(BF16)
    return dot(last[...], jnp.concatenate([once, once], axis=0))


def times_conj(left, right):
    left_re, left_im = left[:, :LANES], left[:, LANES:]
    right_re, right_im = right[:, :LANES], right[:, LANES:]
    return jnp.concatenate(
        [left_re * right_re + left_im * right_im, left_im * right_re - left_re * right_im], axis=1
    )


def signal_grad_kernel(
    blocks, width, pair, unread, first, cosine, sine, second, second_back, last,
    grad_out, cotan_spec, pair_flat, grad_flat,
):
    pair_flat[...] = pair[...].astype(F32)

    def one_group(step, carry):
        channels = [step * GROUP + at for at in range(GROUP)]
        rows = pl.ds(pl.multiple_of(step * (GROUP * blocks), GROUP * blocks), GROUP * blocks)

        def spectrum(offset):
            return to_spectrum(
                pair_flat, channels, blocks, 2 * width, offset, first, cosine, sine, second
            )

        moved = spectrum(0)
        cotan_spec[rows, :] = moved
        grads = from_spectrum(
            times_conj(moved, spectrum(width)), GROUP, blocks, second_back, cosine, sine, last
        )
        for at, channel in enumerate(channels):
            lanes = slice(at * LANES, (at + 1) * LANES)
            grad_flat[channel_rows(channel, blocks, width), :] = grads[:, lanes]
        return carry

    lax.fori_loop(0, width // GROUP, one_group, 0)
    grad_out[...] = grad_flat[...].astype(BF16)


def filter_grad_kernel(
    blocks, width, together, moved, cotan_spec, grad_signal, unread, first, cosine, sine, second,
    second_back, last, bundled, moved_flat, grad_flat,
):
    moved_flat[...] = moved[...].reshape(moved_flat.shape).astype(F32)
    taps = jnp.sum(moved[:, :width, :].astype(F32), axis=0).astype(BF16)
    bundled[:, width : 2 * width, :] = jnp.broadcast_to(taps[None], (blocks, width, LANES))
    terms = moved[:, width:, :].astype(F32) * grad_signal[...].astype(F32)
    sums = jnp.sum(jnp.sum(terms, axis=0), axis=1, keepdims=True)
    high = sums.astype(BF16).astype(F32)
    place = lax.broadcasted_iota(jnp.int32, (width, LANES), 0)
    place = place + lax.rem(lax.axis_index("ctx"), together) * width
    here = lax.broadcasted_iota(jnp.int32, (width, LANES), 1) == place
    lines = [jnp.sum(jnp.where(here, part, 0.0), axis=0) for part in (high, sums - high)]
    row = lax.broadcasted_iota(jnp.int32, (EXTRA, LANES), 0)
    lines = jnp.where(row == 0, lines[0][None], jnp.where(row == 1, lines[1][None], 0.0))
    bundled[:, 2 * width :, :] = jnp.broadcast_to(
        lines.astype(BF16)[None], (blocks, EXTRA, LANES)
    )

    def one_group(step, carry):
        channels = [step * GROUP + at for at in range(GROUP)]
        spec = to_spectrum(
            moved_flat, channels, blocks, 2 * width, width, first, cosine, sine, second
        )
        rows = pl.ds(pl.multiple_of(step * (GROUP * blocks), GROUP * blocks), GROUP * blocks)
        grads = from_spectrum(
            times_conj(cotan_spec[rows, :], spec), GROUP, blocks, second_back, cosine, sine, last
        )
        for at, channel in enumerate(channels):
            lanes = slice(at * LANES, (at + 1) * LANES)
            grad_flat[channel_rows(channel, blocks, width), :] = grads[:, lanes]
        return carry

    lax.fori_loop(0, width // GROUP, one_group, 0)
    bundled[:, :width, :] = grad_flat[...].reshape(blocks, width, LANES).astype(BF16)


def signal_grad(pair, after, blocks, tables):
    rows = pair.shape[0] // 2
    return by_rows(
        functools.partial(signal_grad_kernel, blocks, rows // blocks), "signal_grad", 1, 1,
        (pair, after, *tables),
        [whole_spec(pair.shape), UNREAD] + [whole_spec(table.shape) for table in tables],
        [((rows, LANES), BF16), ((rows, 2 * LANES), F32)],
        [whole_spec((rows, LANES)), whole_spec((rows, 2 * LANES))],
        [pltpu.VMEM((2 * rows, LANES), F32), pltpu.VMEM((rows, LANES), F32)],
    )


def filter_grad(moved, cotan_spec, grad_signal, after, tables):
    blocks, both, _ = moved.shape
    width = both // 2
    ins = (moved, cotan_spec, grad_signal.reshape(blocks, width, LANES))
    shape = (blocks, 2 * width + EXTRA, LANES)
    return by_rows(
        functools.partial(filter_grad_kernel, blocks, width, LANES // width), "filter_grad", 1, 1,
        (*ins, after, *tables),
        [whole_spec(value.shape) for value in ins]
        + [UNREAD]
        + [whole_spec(table.shape) for table in tables],
        [(shape, BF16)],
        [whole_spec(shape)],
        [pltpu.VMEM((2 * blocks * width, LANES), F32), pltpu.VMEM((blocks * width, LANES), F32)],
    )[0]


def swapped(rows):
    return lax.all_to_all(rows, "ctx", split_axis=0, concat_axis=0, tiled=True)


def parts_over_ch(row):
    count = lax.axis_size("ch")
    routes = [[(i, (i + step) % count) for i in range(count)] for step in range(1, count)]
    return [row] + [lax.ppermute(row, "ch", route) for route in routes]


def shifted(block, distance):
    devices = range(lax.axis_size("ctx"))
    route = [(i - distance, i) for i in devices if i - distance in devices]
    return lax.ppermute(block, "ctx", route)


def local(query_mr, key_mr, value_mr, key_li, cotangent, norm_gain, filter_mr, filter_li):
    blocks = lax.axis_size("ctx")
    rows = query_mr.shape[0]
    short = short_tables()
    long = long_tables(blocks)
    width = rows // blocks
    gain = norm_gain.reshape(-1, LANES)
    moved_pair = swapped(pair_up(cotangent, filter_li, blocks)).reshape(2 * rows, LANES)
    prior = shifted(product_of(key_mr, value_mr), 1)
    grad_moved, cotan_spec = signal_grad(moved_pair, prior, blocks, long)
    grad_signal = swapped(grad_moved)
    conv, mixed, window_spec, taps_spec, squares = mr_forward(
        key_mr, value_mr, prior, query_mr, filter_mr, grad_moved, short
    )
    squares = parts_over_ch(squares)
    grad_key_li, terms = mr_project(grad_signal, key_li, mixed, gain, squares)
    project = parts_over_ch(terms)
    taps_and_signal, spec = taps_grad_of(
        grad_signal, key_li, mixed, query_mr, gain, window_spec, short, project, squares, blocks
    )
    moved = swapped(taps_and_signal)
    grad_query, before_grad, own_grad = product_grad_of(
        grad_signal, key_li, mixed, conv, gain, spec, taps_spec, short, project, squares
    )
    after = shifted(before_grad, -1)
    grad_product = own_grad + after.astype(F32)
    grad_key = (grad_product * value_mr.astype(F32)).astype(BF16)
    grad_value = (grad_product * key_mr.astype(F32)).astype(BF16)
    bundled = filter_grad(moved, cotan_spec, grad_moved, after, long)
    grad_filter_li, grad_filter_mr, gain_rows = deliver(swapped(bundled), gain, blocks, width)
    grad_gain = gain_rows.reshape(rows)
    return (
        grad_query,
        grad_key,
        grad_value,
        grad_key_li,
        grad_gain,
        grad_filter_mr,
        grad_filter_li,
    )


def solution(mesh):
    in_specs = (
        P("ch", "ctx"),
        P("ch", "ctx"),
        P("ch", "ctx"),
        P("ch", "ctx"),
        P("ch", "ctx"),
        P("ch"),
        P("ch", None),
        P("ch", "ctx"),
    )
    out_specs = (
        P("ch", "ctx"),
        P("ch", "ctx"),
        P("ch", "ctx"),
        P("ch", "ctx"),
        P("ch"),
        P("ch", None),
        P("ch", "ctx"),
    )
    return jax.shard_map(local, mesh=mesh, in_specs=in_specs, out_specs=out_specs, check_vma=False)
```

```python
import functools
import math

import jax
import jax.numpy as jnp
import numpy as np
from jax import lax
from jax.experimental import pallas as pl
from jax.experimental.pallas import tpu as pltpu
from jax.sharding import PartitionSpec as P

D = 8192
LANES = 128
EPSILON = 1e-06
BF16 = jnp.bfloat16
F32 = jnp.float32


def halves(table):
    high = table.astype(np.float32).astype(BF16)
    low = (table - high.astype(np.float64)).astype(np.float32).astype(BF16)
    return jnp.asarray(high), jnp.asarray(low)


def short_tables():
    place = np.arange(2 * LANES)
    angle = 2.0 * math.pi / (2 * LANES) * place[:, None] * (np.arange(LANES)[None, :] + 0.5)
    ahead = np.concatenate([np.cos(angle), -np.sin(angle)], axis=1)
    return halves(ahead) + halves(ahead.T / LANES)


def long_tables(blocks):
    radix = 2 * blocks
    total = radix * LANES
    half = np.arange(blocks) + 0.5
    outer = 2.0 * math.pi / radix * half[:, None] * np.arange(blocks)[None, :]
    first = np.concatenate([np.cos(outer), -np.sin(outer)], axis=0)
    twist = 2.0 * math.pi / total * half[:, None] * np.arange(LANES)[None, :]
    inner = 2.0 * math.pi / LANES * (np.arange(LANES)[:, None] * np.arange(LANES)[None, :] % LANES)
    cosine, sine = np.cos(inner), np.sin(inner)
    second = np.block([[cosine, -sine], [sine, cosine]])
    first_high, first_low = halves(first)
    last_high, last_low = halves(first.T * (2.0 / total))
    return (
        jnp.concatenate([first_high, first_low], axis=1),
        jnp.asarray(np.cos(twist), F32),
        jnp.asarray(np.sin(twist), F32),
        jnp.asarray(second, BF16),
        jnp.asarray(second.T, BF16),
        jnp.concatenate([last_high, last_low], axis=1),
    )


def dot(left, right):
    return jnp.dot(left, right, preferred_element_type=F32)


def split(values):
    high = values.astype(BF16)
    return high, (values - high.astype(F32)).astype(BF16)


def dot3(values, high, low):
    values_high, values_low = split(values)
    return dot(
        jnp.concatenate([values_high, values_low, values_high], axis=1),
        jnp.concatenate([high, high, low], axis=0),
    )


def dot1(values, table):
    return dot(values.astype(BF16), table)


def dot2(values, high, low):
    once = values.astype(BF16)
    return dot(jnp.concatenate([once, once], axis=1), jnp.concatenate([high, low], axis=0))


def product_kernel(key, value, product):
    product[...] = (key[...].astype(F32) * value[...].astype(F32)).astype(BF16)


def pair_kernel(cotan, filt, pair):
    blocks, both = pair.shape[:2]
    pair[:, : both // 2, :] = cotan[...].reshape(blocks, -1, LANES)
    pair[:, both // 2 :, :] = filt[...].astype(BF16).reshape(blocks, -1, LANES)


def gain_column(gain):
    here = lax.broadcasted_iota(jnp.int32, (LANES, LANES), 0)
    diagonal = here == lax.broadcasted_iota(jnp.int32, (LANES, LANES), 1)
    columns = [
        jnp.sum(jnp.where(diagonal, gain[at : at + 1, :], 0.0), axis=1, keepdims=True)
        for at in range(gain.shape[0])
    ]
    return jnp.concatenate(columns, axis=0)


def mr_forward_kernel(
    key, value, prior, query, taps, unread, ahead_high, ahead_low, back_high, back_low,
    conv_out, mixed_out, window_spec, taps_spec, squares,
):
    product = key[...].astype(F32) * value[...].astype(F32)
    window = jnp.concatenate([prior[...].astype(F32), product], axis=1)
    spec = dot3(window, ahead_high[...], ahead_low[...])
    filt = dot3(taps[...], ahead_high[:LANES], ahead_low[:LANES])
    spec_re, spec_im = spec[:, :LANES], spec[:, LANES:]
    filt_re, filt_im = filt[:, :LANES], filt[:, LANES:]
    passed = jnp.concatenate(
        [spec_re * filt_re - spec_im * filt_im, spec_re * filt_im + spec_im * filt_re], axis=1
    )
    conv = dot3(passed, back_high[:, LANES:], back_low[:, LANES:])
    mixed_bf = (query[...].astype(F32) * conv).astype(BF16)
    mixed = mixed_bf.astype(F32)
    conv_out[...] = conv
    mixed_out[...] = mixed_bf
    window_spec[...] = spec
    taps_spec[...] = filt

    @pl.when(pl.program_id(0) == 0)
    def _():
        squares[...] = jnp.zeros_like(squares)

    squares[...] += jnp.sum(mixed * mixed, axis=0, keepdims=True)


def gain_block(gain, count):
    groups = count // LANES
    return gain_column(gain[pl.ds(pl.program_id(0) * groups, groups), :])


def total(parts):
    return functools.reduce(lambda left, right: left + right, [part[...] for part in parts])


def inverse_rms(squares):
    return lax.rsqrt(total(squares) / D + EPSILON)


def mr_project_kernel(ready, leave, grad_signal, key_li, mixed, gain, *rest):
    squares, grad_key_li, project = rest[:-2], rest[-2], rest[-1]
    ready()
    scaled = mixed[...].astype(F32) * inverse_rms(squares) * gain_column(gain[...])
    grad_scaled = grad_signal[...].astype(F32) * scaled
    project[...] = jnp.sum(grad_scaled * key_li[...].astype(F32), axis=0, keepdims=True)
    leave[1]()
    grad_key_li[...] = grad_scaled.astype(BF16)
    leave[0]()


def against(spec, other):
    spec_re, spec_im = spec[:, :LANES], spec[:, LANES:]
    other_re, other_im = other[:, :LANES], other[:, LANES:]
    return jnp.concatenate(
        [spec_re * other_re + spec_im * other_im, spec_im * other_re - spec_re * other_im], axis=1
    )


def mixed_gradient(grad_signal, key_li, mixed, gain, project, squares):
    inv = inverse_rms(squares)
    normed = mixed[...].astype(F32) * inv
    gated = key_li[...].astype(F32) * gain_block(gain, mixed.shape[0])
    grads = grad_signal[...].astype(F32) * gated - normed * (total(project) / D)
    return inv * grads, normed * gated


def taps_grad_kernel(
    grad_signal, key_li, mixed, query, gain, window_spec,
    ahead_high, ahead_low, back_high, *rest,
):
    count = (len(rest) - 2) // 2
    taps_and_signal, spec_out = rest[-2:]
    grad_mixed, signal = mixed_gradient(
        grad_signal, key_li, mixed, gain, rest[:count], rest[count : 2 * count]
    )
    spec = dot2(
        grad_mixed * query[...].astype(F32), ahead_high[LANES:], ahead_low[LANES:]
    )
    spec_out[...] = spec
    taps_grad = dot1(against(spec, window_spec[...]), back_high[:, :LANES]).astype(BF16)
    blocks, both_widths = taps_and_signal.shape[:2]
    width = both_widths // 2
    taps_and_signal[:, :width, :] = taps_grad.reshape(blocks, width, LANES)
    taps_and_signal[:, width:, :] = signal.astype(BF16).reshape(blocks, width, LANES)


def product_grad_kernel(
    grad_signal, key_li, mixed, conv, gain, spec, taps_spec, back_high, *rest
):
    count = (len(rest) - 3) // 2
    grad_query, before_grad, own_grad = rest[-3:]
    grad_mixed, _ = mixed_gradient(
        grad_signal, key_li, mixed, gain, rest[:count], rest[count : 2 * count]
    )
    grad_query[...] = (grad_mixed * conv[...]).astype(BF16)
    both = dot1(against(spec[...], taps_spec[...]), back_high[...])
    before_grad[...] = both[:, :LANES].astype(BF16)
    own_grad[...] = both[:, LANES:]


UNREAD = pl.BlockSpec(memory_space=pltpu.HBM)
LIMIT = pltpu.CompilerParams(vmem_limit_bytes=60 * 1024 * 1024)
STAGED_LIMIT = pltpu.CompilerParams(vmem_limit_bytes=28 * 1024 * 1024)
PRODUCT_ROWS = 1024
PAIR_ROWS = 1024
FORWARD_ROWS = 1024
BACKWARD_ROWS = 1024


def row_spec(count, width=LANES):
    return pl.BlockSpec((count, width), lambda i: (i, 0))


def whole_spec(shape):
    return pl.BlockSpec(shape, lambda i: (0,) * len(shape))


def by_rows(kernel, name, count, rows, ins, in_specs, outs, out_specs, scratch=()):
    return pl.pallas_call(
        kernel,
        grid=(rows // count,),
        in_specs=in_specs,
        out_specs=out_specs,
        out_shape=[jax.ShapeDtypeStruct(*out) for out in outs],
        scratch_shapes=scratch,
        compiler_params=LIMIT,
        name=name,
    )(*ins)


ROW = ((1, LANES), F32)


def staged(kernel, name, here, fetched, unread, outs, scratch=()):
    counts = [len(here), len(fetched), len(unread), len(outs), len(fetched), len(outs)]

    def body(*refs):
        groups, at = [], 0
        for count in counts:
            groups.append(refs[at : at + count])
            at += count
        near, far, _, far_outs, near_far, near_outs = groups
        rest, arrived, left = refs[at:-2], refs[-2], refs[-1]
        copies = [
            pltpu.make_async_copy(source, target, arrived.at[i])
            for i, (source, target) in enumerate(zip(far, near_far))
        ]
        for copy in copies:
            copy.start()

        def ready():
            for copy in copies:
                copy.wait()

        backs = [
            pltpu.make_async_copy(source, target, left.at[i])
            for i, (source, target) in enumerate(zip(near_outs, far_outs))
        ]
        kernel(ready, [back.start for back in backs], *near, *near_far, *near_outs, *rest)
        for back in backs:
            back.wait()

    return pl.pallas_call(
        body,
        in_specs=[pl.BlockSpec(memory_space=pltpu.VMEM)] * len(here)
        + [UNREAD] * (len(fetched) + len(unread)),
        out_specs=[UNREAD] * len(outs),
        out_shape=[jax.ShapeDtypeStruct(*out) for out in outs],
        scratch_shapes=[pltpu.VMEM(value.shape, value.dtype) for value in fetched]
        + [pltpu.VMEM(*out) for out in outs]
        + list(scratch)
        + [pltpu.SemaphoreType.DMA((len(fetched),)), pltpu.SemaphoreType.DMA((len(outs),))],
        compiler_params=STAGED_LIMIT,
        name=name,
    )(*here, *fetched, *unread)


def product_of(key, value):
    rows = key.shape[0]
    each = row_spec(PRODUCT_ROWS)
    return by_rows(
        product_kernel, "product_of", PRODUCT_ROWS, rows,
        (key, value), [each] * 2, [((rows, LANES), BF16)], [each],
    )[0]


def pair_up(cotan, filt, blocks):
    rows = cotan.shape[0]
    width = rows // blocks
    return by_rows(
        pair_kernel, "pair_up", PAIR_ROWS, rows,
        (cotan, filt), [row_spec(PAIR_ROWS)] * 2,
        [((blocks, 2 * width, LANES), BF16)],
        [pl.BlockSpec((PAIR_ROWS // width, 2 * width, LANES), lambda i: (i, 0, 0))],
    )[0]


def mr_forward(key, value, prior, query, taps, after, tables):
    rows = key.shape[0]
    each, wide = row_spec(FORWARD_ROWS), row_spec(FORWARD_ROWS, 2 * LANES)
    return by_rows(
        mr_forward_kernel, "mr_forward", FORWARD_ROWS, rows,
        (key, value, prior, query, taps, after, *tables),
        [each] * 5 + [UNREAD] + [whole_spec(table.shape) for table in tables],
        [((rows, LANES), F32), ((rows, LANES), BF16)] + [((rows, 2 * LANES), F32)] * 2 + [ROW],
        [each, each, wide, wide, whole_spec((1, LANES))],
    )


def mr_project(grad_signal, key_li, mixed, gain, squares):
    return staged(
        mr_project_kernel, "mr_project", (grad_signal,), (key_li, mixed, gain, *squares), (),
        [(mixed.shape, BF16), ROW],
    )


def taps_grad_of(
    grad_signal, key_li, mixed, query, gain, window_spec, tables, project, squares, blocks
):
    rows = mixed.shape[0]
    width = rows // blocks
    each, wide = row_spec(BACKWARD_ROWS), row_spec(BACKWARD_ROWS, 2 * LANES)
    return by_rows(
        taps_grad_kernel, "taps_grad_of", BACKWARD_ROWS, rows,
        (grad_signal, key_li, mixed, query, gain, window_spec, *tables[:3], *project, *squares),
        [each] * 4
        + [whole_spec(gain.shape), wide]
        + [whole_spec(table.shape) for table in tables[:3]]
        + [whole_spec((1, LANES))] * (len(project) + len(squares)),
        [((blocks, 2 * width, LANES), BF16), ((rows, 2 * LANES), F32)],
        [pl.BlockSpec((BACKWARD_ROWS // width, 2 * width, LANES), lambda i: (i, 0, 0)), wide],
    )


def product_grad_of(
    grad_signal, key_li, mixed, conv, gain, spec, taps_spec, tables, project, squares
):
    rows = mixed.shape[0]
    each, wide = row_spec(BACKWARD_ROWS), row_spec(BACKWARD_ROWS, 2 * LANES)
    return by_rows(
        product_grad_kernel, "product_grad_of", BACKWARD_ROWS, rows,
        (
            grad_signal, key_li, mixed, conv, gain, spec, taps_spec, tables[2],
            *project, *squares,
        ),
        [each] * 4
        + [whole_spec(gain.shape), wide, wide, whole_spec(tables[2].shape)]
        + [whole_spec((1, LANES))] * (len(project) + len(squares)),
        [((rows, LANES), BF16)] * 2 + [((rows, LANES), F32)],
        [each] * 3,
    )


def deliver_kernel(ready, leave, bundled, gain, filter_grad, taps_grad, gain_grad):
    blocks = bundled.shape[0]
    width = filter_grad.shape[0] // blocks
    filter_grad[...] = bundled[:, :width, :].astype(F32).reshape(filter_grad.shape)
    leave[0]()
    taps_grad[...] = bundled[:, width : 2 * width, :].astype(F32).reshape(taps_grad.shape)
    leave[1]()
    together = LANES // width
    row = lax.broadcasted_iota(jnp.int32, (gain.shape[0], blocks), 0)
    block = lax.broadcasted_iota(jnp.int32, (gain.shape[0], blocks), 1)
    own = jnp.where((block >= row * together) & (block < (row + 1) * together), 1.0, 0.0)
    own = own.astype(BF16)
    lines = bundled[:, 2 * width :, :].astype(F32)
    high, low = lines[:, 0, :].astype(BF16), lines[:, 1, :].astype(BF16)
    ready()
    gain_grad[...] = (dot(own, high) + dot(own, low)) / gain[...]
    leave[2]()


def deliver(bundled, gain, blocks, width):
    return staged(
        deliver_kernel, "deliver", (bundled,), (gain,), (),
        [((blocks * width, LANES), F32)] * 2 + [(gain.shape, F32)],
    )


EXTRA = 8
GROUP = 16


def channel_rows(channel, blocks, width):
    return pl.ds(channel, blocks, stride=width)


def to_spectrum(flat, channels, blocks, width, offset, first, cosine, sine, second):
    pieces = [flat[channel_rows(offset + c, blocks, width), :].astype(BF16) for c in channels]
    grid = jnp.concatenate(pieces, axis=1)
    outer = dot(first[...], jnp.concatenate([grid, grid], axis=0))
    cos, sin = cosine[...], sine[...]
    turned = []
    for at in range(len(channels)):
        lanes = slice(at * LANES, (at + 1) * LANES)
        real, imag = outer[:blocks, lanes], outer[blocks:, lanes]
        turned.append(
            jnp.concatenate([real * cos + imag * sin, imag * cos - real * sin], axis=1)
        )
    return dot1(jnp.concatenate(turned, axis=0), second[...])


def from_spectrum(spec, count, blocks, second, cosine, sine, last):
    inner = dot1(spec, second[...])
    cos, sin = cosine[...], sine[...]
    turned = []
    for at in range(count):
        rows = slice(at * blocks, (at + 1) * blocks)
        real, imag = inner[rows, :LANES], inner[rows, LANES:]
        turned.append(
            jnp.concatenate([real * cos - imag * sin, imag * cos + real * sin], axis=0)
        )
    once = jnp.concatenate(turned, axis=1).astype(BF16)
    return dot(last[...], jnp.concatenate([once, once], axis=0))


def times_conj(left, right):
    left_re, left_im = left[:, :LANES], left[:, LANES:]
    right_re, right_im = right[:, :LANES], right[:, LANES:]
    return jnp.concatenate(
        [left_re * right_re + left_im * right_im, left_im * right_re - left_re * right_im], axis=1
    )


def signal_grad_kernel(
    blocks, width, ready, leave, pair, first, cosine, sine, second, second_back, last,
    grad_out, cotan_spec, pair_flat, grad_flat,
):
    pair_flat[...] = pair[...].astype(F32)
    ready()

    def one_group(step, carry):
        channels = [step * GROUP + at for at in range(GROUP)]
        rows = pl.ds(pl.multiple_of(step * (GROUP * blocks), GROUP * blocks), GROUP * blocks)

        def spectrum(offset):
            return to_spectrum(
                pair_flat, channels, blocks, 2 * width, offset, first, cosine, sine, second
            )

        moved = spectrum(0)
        cotan_spec[rows, :] = moved
        grads = from_spectrum(
            times_conj(moved, spectrum(width)), GROUP, blocks, second_back, cosine, sine, last
        )
        for at, channel in enumerate(channels):
            lanes = slice(at * LANES, (at + 1) * LANES)
            grad_flat[channel_rows(channel, blocks, width), :] = grads[:, lanes]
        return carry

    lax.fori_loop(0, width // GROUP, one_group, 0)
    grad_out[...] = grad_flat[...].astype(BF16)
    leave[0]()
    leave[1]()


def filter_grad_kernel(
    blocks, width, together, ready, leave, moved, cotan_spec, grad_signal, first, cosine, sine,
    second, second_back, last, bundled, moved_flat, grad_flat,
):
    moved_flat[...] = moved[...].reshape(moved_flat.shape).astype(F32)
    taps = jnp.sum(moved[:, :width, :].astype(F32), axis=0).astype(BF16)
    bundled[:, width : 2 * width, :] = jnp.broadcast_to(taps[None], (blocks, width, LANES))
    ready()
    terms = moved[:, width:, :].astype(F32) * grad_signal[...].astype(F32)
    sums = jnp.sum(jnp.sum(terms, axis=0), axis=1, keepdims=True)
    high = sums.astype(BF16).astype(F32)
    place = lax.broadcasted_iota(jnp.int32, (width, LANES), 0)
    place = place + lax.rem(lax.axis_index("ctx"), together) * width
    here = lax.broadcasted_iota(jnp.int32, (width, LANES), 1) == place
    lines = [jnp.sum(jnp.where(here, part, 0.0), axis=0) for part in (high, sums - high)]
    row = lax.broadcasted_iota(jnp.int32, (EXTRA, LANES), 0)
    lines = jnp.where(row == 0, lines[0][None], jnp.where(row == 1, lines[1][None], 0.0))
    bundled[:, 2 * width :, :] = jnp.broadcast_to(
        lines.astype(BF16)[None], (blocks, EXTRA, LANES)
    )

    def one_group(step, carry):
        channels = [step * GROUP + at for at in range(GROUP)]
        spec = to_spectrum(
            moved_flat, channels, blocks, 2 * width, width, first, cosine, sine, second
        )
        rows = pl.ds(pl.multiple_of(step * (GROUP * blocks), GROUP * blocks), GROUP * blocks)
        grads = from_spectrum(
            times_conj(cotan_spec[rows, :], spec), GROUP, blocks, second_back, cosine, sine, last
        )
        for at, channel in enumerate(channels):
            lanes = slice(at * LANES, (at + 1) * LANES)
            grad_flat[channel_rows(channel, blocks, width), :] = grads[:, lanes]
        return carry

    lax.fori_loop(0, width // GROUP, one_group, 0)
    bundled[:, :width, :] = grad_flat[...].reshape(blocks, width, LANES).astype(BF16)
    leave[0]()


def signal_grad(pair, after, blocks, tables):
    rows = pair.shape[0] // 2
    return staged(
        functools.partial(signal_grad_kernel, blocks, rows // blocks), "signal_grad",
        (pair,), tables, (after,),
        [((rows, LANES), BF16), ((rows, 2 * LANES), F32)],
        [pltpu.VMEM((2 * rows, LANES), F32), pltpu.VMEM((rows, LANES), F32)],
    )


def filter_grad(moved, cotan_spec, grad_signal, after, tables):
    blocks, both, _ = moved.shape
    width = both // 2
    return staged(
        functools.partial(filter_grad_kernel, blocks, width, LANES // width), "filter_grad",
        (moved,), (cotan_spec, grad_signal.reshape(blocks, width, LANES), *tables), (after,),
        [((blocks, 2 * width + EXTRA, LANES), BF16)],
        [pltpu.VMEM((2 * blocks * width, LANES), F32), pltpu.VMEM((blocks * width, LANES), F32)],
    )[0]


def swapped(rows):
    return lax.all_to_all(rows, "ctx", split_axis=0, concat_axis=0, tiled=True)


def parts_over_ch(row):
    count = lax.axis_size("ch")
    routes = [[(i, (i + step) % count) for i in range(count)] for step in range(1, count)]
    return [row] + [lax.ppermute(row, "ch", route) for route in routes]


def shifted(block, distance):
    devices = range(lax.axis_size("ctx"))
    route = [(i - distance, i) for i in devices if i - distance in devices]
    return lax.ppermute(block, "ctx", route)


def local(query_mr, key_mr, value_mr, key_li, cotangent, norm_gain, filter_mr, filter_li):
    blocks = lax.axis_size("ctx")
    rows = query_mr.shape[0]
    short = short_tables()
    long = long_tables(blocks)
    width = rows // blocks
    gain = norm_gain.reshape(-1, LANES)
    moved_pair = swapped(pair_up(cotangent, filter_li, blocks)).reshape(2 * rows, LANES)
    prior = shifted(product_of(key_mr, value_mr), 1)
    grad_moved, cotan_spec = signal_grad(moved_pair, prior, blocks, long)
    grad_signal = swapped(grad_moved)
    conv, mixed, window_spec, taps_spec, squares = mr_forward(
        key_mr, value_mr, prior, query_mr, filter_mr, grad_moved, short
    )
    squares = parts_over_ch(squares)
    grad_key_li, terms = mr_project(grad_signal, key_li, mixed, gain, squares)
    project = parts_over_ch(terms)
    taps_and_signal, spec = taps_grad_of(
        grad_signal, key_li, mixed, query_mr, gain, window_spec, short, project, squares, blocks
    )
    moved = swapped(taps_and_signal)
    grad_query, before_grad, own_grad = product_grad_of(
        grad_signal, key_li, mixed, conv, gain, spec, taps_spec, short, project, squares
    )
    after = shifted(before_grad, -1)
    grad_product = own_grad + after.astype(F32)
    grad_key = (grad_product * value_mr.astype(F32)).astype(BF16)
    grad_value = (grad_product * key_mr.astype(F32)).astype(BF16)
    bundled = filter_grad(moved, cotan_spec, grad_moved, after, long)
    grad_filter_li, grad_filter_mr, gain_rows = deliver(swapped(bundled), gain, blocks, width)
    grad_gain = gain_rows.reshape(rows)
    return (
        grad_query,
        grad_key,
        grad_value,
        grad_key_li,
        grad_gain,
        grad_filter_mr,
        grad_filter_li,
    )


def solution(mesh):
    in_specs = (
        P("ch", "ctx"),
        P("ch", "ctx"),
        P("ch", "ctx"),
        P("ch", "ctx"),
        P("ch", "ctx"),
        P("ch"),
        P("ch", None),
        P("ch", "ctx"),
    )
    out_specs = (
        P("ch", "ctx"),
        P("ch", "ctx"),
        P("ch", "ctx"),
        P("ch", "ctx"),
        P("ch"),
        P("ch", None),
        P("ch", "ctx"),
    )
    return jax.shard_map(local, mesh=mesh, in_specs=in_specs, out_specs=out_specs, check_vma=False)
```

```python
import functools
import math

import jax
import jax.numpy as jnp
import numpy as np
from jax import lax
from jax.experimental import pallas as pl
from jax.experimental.pallas import tpu as pltpu
from jax.sharding import PartitionSpec as P

D = 8192
LANES = 128
EPSILON = 1e-06
BF16 = jnp.bfloat16
F32 = jnp.float32


def halves(table):
    high = table.astype(np.float32).astype(BF16)
    low = (table - high.astype(np.float64)).astype(np.float32).astype(BF16)
    return jnp.asarray(high), jnp.asarray(low)


def short_tables():
    place = np.arange(2 * LANES)
    angle = 2.0 * math.pi / (2 * LANES) * place[:, None] * (np.arange(LANES)[None, :] + 0.5)
    ahead = np.concatenate([np.cos(angle), -np.sin(angle)], axis=1)
    return halves(ahead) + halves(ahead.T / LANES)


def long_tables(blocks):
    radix = 2 * blocks
    total = radix * LANES
    half = np.arange(blocks) + 0.5
    outer = 2.0 * math.pi / radix * half[:, None] * np.arange(blocks)[None, :]
    first = np.concatenate([np.cos(outer), -np.sin(outer)], axis=0)
    twist = 2.0 * math.pi / total * half[:, None] * np.arange(LANES)[None, :]
    inner = 2.0 * math.pi / LANES * (np.arange(LANES)[:, None] * np.arange(LANES)[None, :] % LANES)
    cosine, sine = np.cos(inner), np.sin(inner)
    second = np.block([[cosine, -sine], [sine, cosine]])
    first_high, first_low = halves(first)
    last_high, last_low = halves(first.T * (2.0 / total))
    return (
        jnp.concatenate([first_high, first_low], axis=1),
        jnp.asarray(np.cos(twist), F32),
        jnp.asarray(np.sin(twist), F32),
        jnp.asarray(second, BF16),
        jnp.asarray(second.T, BF16),
        jnp.concatenate([last_high, last_low], axis=1),
    )


def dot(left, right):
    return jnp.dot(left, right, preferred_element_type=F32)


def split(values):
    high = values.astype(BF16)
    return high, (values - high.astype(F32)).astype(BF16)


def dot3(values, high, low):
    values_high, values_low = split(values)
    return dot(
        jnp.concatenate([values_high, values_low, values_high], axis=1),
        jnp.concatenate([high, high, low], axis=0),
    )


def dot1(values, table):
    return dot(values.astype(BF16), table)


def dot2(values, high, low):
    once = values.astype(BF16)
    return dot(jnp.concatenate([once, once], axis=1), jnp.concatenate([high, low], axis=0))


def product_kernel(key, value, product):
    product[...] = (key[...].astype(F32) * value[...].astype(F32)).astype(BF16)


def pair_kernel(cotan, filt, pair):
    blocks, both = pair.shape[:2]
    pair[:, : both // 2, :] = cotan[...].reshape(blocks, -1, LANES)
    pair[:, both // 2 :, :] = filt[...].astype(BF16).reshape(blocks, -1, LANES)


def gain_column(gain):
    here = lax.broadcasted_iota(jnp.int32, (LANES, LANES), 0)
    diagonal = here == lax.broadcasted_iota(jnp.int32, (LANES, LANES), 1)
    columns = [
        jnp.sum(jnp.where(diagonal, gain[at : at + 1, :], 0.0), axis=1, keepdims=True)
        for at in range(gain.shape[0])
    ]
    return jnp.concatenate(columns, axis=0)


def mr_forward_kernel(
    key, value, prior, query, taps, unread, ahead_high, ahead_low, back_high, back_low,
    conv_out, mixed_out, window_spec, taps_spec, squares,
):
    product = key[...].astype(F32) * value[...].astype(F32)
    window = jnp.concatenate([prior[...].astype(F32), product], axis=1)
    spec = dot3(window, ahead_high[...], ahead_low[...])
    filt = dot3(taps[...], ahead_high[:LANES], ahead_low[:LANES])
    spec_re, spec_im = spec[:, :LANES], spec[:, LANES:]
    filt_re, filt_im = filt[:, :LANES], filt[:, LANES:]
    passed = jnp.concatenate(
        [spec_re * filt_re - spec_im * filt_im, spec_re * filt_im + spec_im * filt_re], axis=1
    )
    conv = dot3(passed, back_high[:, LANES:], back_low[:, LANES:])
    mixed_bf = (query[...].astype(F32) * conv).astype(BF16)
    mixed = mixed_bf.astype(F32)
    conv_out[...] = conv
    mixed_out[...] = mixed_bf
    window_spec[...] = spec
    taps_spec[...] = filt

    @pl.when(pl.program_id(0) == 0)
    def _():
        squares[...] = jnp.zeros_like(squares)

    squares[...] += jnp.sum(mixed * mixed, axis=0, keepdims=True)


def gain_block(gain, count):
    groups = count // LANES
    return gain_column(gain[pl.ds(pl.program_id(0) * groups, groups), :])


def total(parts):
    return functools.reduce(lambda left, right: left + right, [part[...] for part in parts])


def inverse_rms(squares):
    return lax.rsqrt(total(squares) / D + EPSILON)


def mr_project_kernel(ready, leave, grad_signal, key_li, mixed, gain, *rest):
    squares, grad_key_li, project = rest[:-2], rest[-2], rest[-1]
    ready()
    scaled = mixed[...].astype(F32) * inverse_rms(squares) * gain_column(gain[...])
    grad_scaled = grad_signal[...].astype(F32) * scaled
    project[...] = jnp.sum(grad_scaled * key_li[...].astype(F32), axis=0, keepdims=True)
    leave[1]()
    grad_key_li[...] = grad_scaled.astype(BF16)
    leave[0]()


def against(spec, other):
    spec_re, spec_im = spec[:, :LANES], spec[:, LANES:]
    other_re, other_im = other[:, :LANES], other[:, LANES:]
    return jnp.concatenate(
        [spec_re * other_re + spec_im * other_im, spec_im * other_re - spec_re * other_im], axis=1
    )


def mixed_gradient(grad_signal, key_li, mixed, gain, project, squares):
    inv = inverse_rms(squares)
    normed = mixed[...].astype(F32) * inv
    gated = key_li[...].astype(F32) * gain_block(gain, mixed.shape[0])
    grads = grad_signal[...].astype(F32) * gated - normed * (total(project) / D)
    return inv * grads, normed * gated


def taps_grad_kernel(
    grad_signal, key_li, mixed, query, gain, window_spec,
    ahead_high, ahead_low, back_high, *rest,
):
    count = (len(rest) - 2) // 2
    taps_and_signal, spec_out = rest[-2:]
    grad_mixed, signal = mixed_gradient(
        grad_signal, key_li, mixed, gain, rest[:count], rest[count : 2 * count]
    )
    spec = dot2(
        grad_mixed * query[...].astype(F32), ahead_high[LANES:], ahead_low[LANES:]
    )
    spec_out[...] = spec
    taps_grad = dot1(against(spec, window_spec[...]), back_high[:, :LANES]).astype(BF16)
    blocks, both_widths = taps_and_signal.shape[:2]
    width = both_widths // 2
    taps_and_signal[:, :width, :] = taps_grad.reshape(blocks, width, LANES)
    taps_and_signal[:, width:, :] = signal.astype(BF16).reshape(blocks, width, LANES)


def product_grad_kernel(
    grad_signal, key_li, mixed, conv, gain, spec, taps_spec, back_high, *rest
):
    count = (len(rest) - 3) // 2
    grad_query, before_grad, own_grad = rest[-3:]
    grad_mixed, _ = mixed_gradient(
        grad_signal, key_li, mixed, gain, rest[:count], rest[count : 2 * count]
    )
    grad_query[...] = (grad_mixed * conv[...]).astype(BF16)
    both = dot1(against(spec[...], taps_spec[...]), back_high[...])
    before_grad[...] = both[:, :LANES].astype(BF16)
    own_grad[...] = both[:, LANES:]


UNREAD = pl.BlockSpec(memory_space=pltpu.HBM)
LIMIT = pltpu.CompilerParams(vmem_limit_bytes=60 * 1024 * 1024)
STAGED_LIMIT = pltpu.CompilerParams(vmem_limit_bytes=28 * 1024 * 1024)
PRODUCT_ROWS = 1024
PAIR_ROWS = 1024
FORWARD_ROWS = 1024
BACKWARD_ROWS = 1024


def row_spec(count, width=LANES):
    return pl.BlockSpec((count, width), lambda i: (i, 0))


def whole_spec(shape):
    return pl.BlockSpec(shape, lambda i: (0,) * len(shape))


def by_rows(kernel, name, count, rows, ins, in_specs, outs, out_specs, scratch=()):
    return pl.pallas_call(
        kernel,
        grid=(rows // count,),
        in_specs=in_specs,
        out_specs=out_specs,
        out_shape=[jax.ShapeDtypeStruct(*out) for out in outs],
        scratch_shapes=scratch,
        compiler_params=LIMIT,
        name=name,
    )(*ins)


ROW = ((1, LANES), F32)


def staged(kernel, name, here, fetched, unread, outs, scratch=()):
    counts = [len(here), len(fetched), len(unread), len(outs), len(fetched), len(outs)]

    def body(*refs):
        groups, at = [], 0
        for count in counts:
            groups.append(refs[at : at + count])
            at += count
        near, far, _, far_outs, near_far, near_outs = groups
        rest, arrived, left = refs[at:-2], refs[-2], refs[-1]
        copies = [
            pltpu.make_async_copy(source, target, arrived.at[i])
            for i, (source, target) in enumerate(zip(far, near_far))
        ]
        for copy in copies:
            copy.start()

        def ready():
            for copy in copies:
                copy.wait()

        backs = [
            pltpu.make_async_copy(source, target, left.at[i])
            for i, (source, target) in enumerate(zip(near_outs, far_outs))
        ]
        kernel(ready, [back.start for back in backs], *near, *near_far, *near_outs, *rest)
        for back in backs:
            back.wait()

    return pl.pallas_call(
        body,
        in_specs=[pl.BlockSpec(memory_space=pltpu.VMEM)] * len(here)
        + [UNREAD] * (len(fetched) + len(unread)),
        out_specs=[UNREAD] * len(outs),
        out_shape=[jax.ShapeDtypeStruct(*out) for out in outs],
        scratch_shapes=[pltpu.VMEM(value.shape, value.dtype) for value in fetched]
        + [pltpu.VMEM(*out) for out in outs]
        + list(scratch)
        + [pltpu.SemaphoreType.DMA((len(fetched),)), pltpu.SemaphoreType.DMA((len(outs),))],
        compiler_params=STAGED_LIMIT,
        name=name,
    )(*here, *fetched, *unread)


def product_of(key, value):
    rows = key.shape[0]
    each = row_spec(PRODUCT_ROWS)
    return by_rows(
        product_kernel, "product_of", PRODUCT_ROWS, rows,
        (key, value), [each] * 2, [((rows, LANES), BF16)], [each],
    )[0]


def pair_up(cotan, filt, blocks):
    rows = cotan.shape[0]
    width = rows // blocks
    return by_rows(
        pair_kernel, "pair_up", PAIR_ROWS, rows,
        (cotan, filt), [row_spec(PAIR_ROWS)] * 2,
        [((blocks, 2 * width, LANES), BF16)],
        [pl.BlockSpec((PAIR_ROWS // width, 2 * width, LANES), lambda i: (i, 0, 0))],
    )[0]


def mr_forward(key, value, prior, query, taps, after, tables):
    rows = key.shape[0]
    each, wide = row_spec(FORWARD_ROWS), row_spec(FORWARD_ROWS, 2 * LANES)
    return by_rows(
        mr_forward_kernel, "mr_forward", FORWARD_ROWS, rows,
        (key, value, prior, query, taps, after, *tables),
        [each] * 5 + [UNREAD] + [whole_spec(table.shape) for table in tables],
        [((rows, LANES), F32), ((rows, LANES), BF16)] + [((rows, 2 * LANES), F32)] * 2 + [ROW],
        [each, each, wide, wide, whole_spec((1, LANES))],
    )


def mr_project(grad_signal, key_li, mixed, gain, squares):
    return staged(
        mr_project_kernel, "mr_project", (grad_signal,), (key_li, mixed, gain, *squares), (),
        [(mixed.shape, BF16), ROW],
    )


def taps_grad_of(
    grad_signal, key_li, mixed, query, gain, window_spec, tables, project, squares, blocks
):
    rows = mixed.shape[0]
    width = rows // blocks
    each, wide = row_spec(BACKWARD_ROWS), row_spec(BACKWARD_ROWS, 2 * LANES)
    return by_rows(
        taps_grad_kernel, "taps_grad_of", BACKWARD_ROWS, rows,
        (grad_signal, key_li, mixed, query, gain, window_spec, *tables[:3], *project, *squares),
        [each] * 4
        + [whole_spec(gain.shape), wide]
        + [whole_spec(table.shape) for table in tables[:3]]
        + [whole_spec((1, LANES))] * (len(project) + len(squares)),
        [((blocks, 2 * width, LANES), BF16), ((rows, 2 * LANES), F32)],
        [pl.BlockSpec((BACKWARD_ROWS // width, 2 * width, LANES), lambda i: (i, 0, 0)), wide],
    )


def product_grad_of(
    grad_signal, key_li, mixed, conv, gain, spec, taps_spec, tables, project, squares
):
    rows = mixed.shape[0]
    each, wide = row_spec(BACKWARD_ROWS), row_spec(BACKWARD_ROWS, 2 * LANES)
    return by_rows(
        product_grad_kernel, "product_grad_of", BACKWARD_ROWS, rows,
        (
            grad_signal, key_li, mixed, conv, gain, spec, taps_spec, tables[2],
            *project, *squares,
        ),
        [each] * 4
        + [whole_spec(gain.shape), wide, wide, whole_spec(tables[2].shape)]
        + [whole_spec((1, LANES))] * (len(project) + len(squares)),
        [((rows, LANES), BF16)] * 2 + [((rows, LANES), F32)],
        [each] * 3,
    )


def deliver_kernel(ready, leave, bundled, gain, filter_grad, taps_grad, gain_grad):
    blocks = bundled.shape[0]
    width = filter_grad.shape[0] // blocks
    filter_grad[...] = bundled[:, :width, :].astype(F32).reshape(filter_grad.shape)
    leave[0]()
    taps_grad[...] = bundled[:, width : 2 * width, :].astype(F32).reshape(taps_grad.shape)
    leave[1]()
    together = LANES // width
    row = lax.broadcasted_iota(jnp.int32, (gain.shape[0], blocks), 0)
    block = lax.broadcasted_iota(jnp.int32, (gain.shape[0], blocks), 1)
    own = jnp.where((block >= row * together) & (block < (row + 1) * together), 1.0, 0.0)
    own = own.astype(BF16)
    lines = bundled[:, 2 * width :, :].astype(F32)
    high, low = lines[:, 0, :].astype(BF16), lines[:, 1, :].astype(BF16)
    ready()
    gain_grad[...] = (dot(own, high) + dot(own, low)) / gain[...]
    leave[2]()


def deliver(bundled, gain, blocks, width):
    return staged(
        deliver_kernel, "deliver", (bundled,), (gain,), (),
        [((blocks * width, LANES), F32)] * 2 + [(gain.shape, F32)],
    )


EXTRA = 8
GROUP = 16


def channel_rows(channel, blocks, width):
    return pl.ds(channel, blocks, stride=width)


def to_spectrum(flat, channels, blocks, width, offset, first, cosine, sine, second):
    pieces = [flat[channel_rows(offset + c, blocks, width), :].astype(BF16) for c in channels]
    grid = jnp.concatenate(pieces, axis=1)
    outer = dot(first[...], jnp.concatenate([grid, grid], axis=0))
    cos, sin = cosine[...], sine[...]
    turned = []
    for at in range(len(channels)):
        lanes = slice(at * LANES, (at + 1) * LANES)
        real, imag = outer[:blocks, lanes], outer[blocks:, lanes]
        turned.append(
            jnp.concatenate([real * cos + imag * sin, imag * cos - real * sin], axis=1)
        )
    return dot1(jnp.concatenate(turned, axis=0), second[...])


def from_spectrum(spec, count, blocks, second, cosine, sine, last):
    inner = dot1(spec, second[...])
    cos, sin = cosine[...], sine[...]
    turned = []
    for at in range(count):
        rows = slice(at * blocks, (at + 1) * blocks)
        real, imag = inner[rows, :LANES], inner[rows, LANES:]
        turned.append(
            jnp.concatenate([real * cos - imag * sin, imag * cos + real * sin], axis=0)
        )
    once = jnp.concatenate(turned, axis=1).astype(BF16)
    return dot(last[...], jnp.concatenate([once, once], axis=0))


def times_conj(left, right):
    left_re, left_im = left[:, :LANES], left[:, LANES:]
    right_re, right_im = right[:, :LANES], right[:, LANES:]
    return jnp.concatenate(
        [left_re * right_re + left_im * right_im, left_im * right_re - left_re * right_im], axis=1
    )


def signal_grad_kernel(
    blocks, width, ready, leave, pair, first, cosine, sine, second, second_back, last,
    grad_out, cotan_spec, pair_flat, grad_flat,
):
    pair_flat[...] = pair[...].astype(F32)
    ready()

    def one_group(step, carry):
        channels = [step * GROUP + at for at in range(GROUP)]
        rows = pl.ds(pl.multiple_of(step * (GROUP * blocks), GROUP * blocks), GROUP * blocks)

        def spectrum(offset):
            return to_spectrum(
                pair_flat, channels, blocks, 2 * width, offset, first, cosine, sine, second
            )

        moved = spectrum(0)
        cotan_spec[rows, :] = moved
        grads = from_spectrum(
            times_conj(moved, spectrum(width)), GROUP, blocks, second_back, cosine, sine, last
        )
        for at, channel in enumerate(channels):
            lanes = slice(at * LANES, (at + 1) * LANES)
            grad_flat[channel_rows(channel, blocks, width), :] = grads[:, lanes]
        return carry

    lax.fori_loop(0, width // GROUP, one_group, 0)
    grad_out[...] = grad_flat[...].astype(BF16)
    leave[0]()
    leave[1]()


def filter_grad_kernel(
    blocks, width, together, ready, leave, moved, cotan_spec, grad_signal, first, cosine, sine,
    second, second_back, last, bundled, moved_flat, grad_flat,
):
    moved_flat[...] = moved[...].reshape(moved_flat.shape).astype(F32)
    taps = jnp.sum(moved[:, :width, :].astype(F32), axis=0).astype(BF16)
    bundled[:, width : 2 * width, :] = jnp.broadcast_to(taps[None], (blocks, width, LANES))
    ready()
    terms = moved[:, width:, :].astype(F32) * grad_signal[...].astype(F32)
    sums = jnp.sum(jnp.sum(terms, axis=0), axis=1, keepdims=True)
    high = sums.astype(BF16).astype(F32)
    place = lax.broadcasted_iota(jnp.int32, (width, LANES), 0)
    place = place + lax.rem(lax.axis_index("ctx"), together) * width
    here = lax.broadcasted_iota(jnp.int32, (width, LANES), 1) == place
    lines = [jnp.sum(jnp.where(here, part, 0.0), axis=0) for part in (high, sums - high)]
    row = lax.broadcasted_iota(jnp.int32, (EXTRA, LANES), 0)
    lines = jnp.where(row == 0, lines[0][None], jnp.where(row == 1, lines[1][None], 0.0))
    bundled[:, 2 * width :, :] = jnp.broadcast_to(
        lines.astype(BF16)[None], (blocks, EXTRA, LANES)
    )

    def one_group(step, carry):
        channels = [step * GROUP + at for at in range(GROUP)]
        spec = to_spectrum(
            moved_flat, channels, blocks, 2 * width, width, first, cosine, sine, second
        )
        rows = pl.ds(pl.multiple_of(step * (GROUP * blocks), GROUP * blocks), GROUP * blocks)
        grads = from_spectrum(
            times_conj(cotan_spec[rows, :], spec), GROUP, blocks, second_back, cosine, sine, last
        )
        for at, channel in enumerate(channels):
            lanes = slice(at * LANES, (at + 1) * LANES)
            grad_flat[channel_rows(channel, blocks, width), :] = grads[:, lanes]
        return carry

    lax.fori_loop(0, width // GROUP, one_group, 0)
    bundled[:, :width, :] = grad_flat[...].reshape(blocks, width, LANES).astype(BF16)
    leave[0]()


def signal_grad(pair, after, blocks, tables):
    rows = pair.shape[0] // 2
    return staged(
        functools.partial(signal_grad_kernel, blocks, rows // blocks), "signal_grad",
        (pair,), tables, (after,),
        [((rows, LANES), BF16), ((rows, 2 * LANES), F32)],
        [pltpu.VMEM((2 * rows, LANES), F32), pltpu.VMEM((rows, LANES), F32)],
    )


def filter_grad(moved, cotan_spec, grad_signal, after, tables):
    blocks, both, _ = moved.shape
    width = both // 2
    return staged(
        functools.partial(filter_grad_kernel, blocks, width, LANES // width), "filter_grad",
        (moved,), (cotan_spec, grad_signal.reshape(blocks, width, LANES), *tables), (after,),
        [((blocks, 2 * width + EXTRA, LANES), BF16)],
        [pltpu.VMEM((2 * blocks * width, LANES), F32), pltpu.VMEM((blocks * width, LANES), F32)],
    )[0]


def swapped(rows):
    return lax.all_to_all(rows, "ctx", split_axis=0, concat_axis=0, tiled=True)


def parts_over_ch(row):
    count = lax.axis_size("ch")
    routes = [[(i, (i + step) % count) for i in range(count)] for step in range(1, count)]
    return [row] + [lax.ppermute(row, "ch", route) for route in routes]


def shifted(block, distance):
    devices = range(lax.axis_size("ctx"))
    route = [(i - distance, i) for i in devices if i - distance in devices]
    return lax.ppermute(block, "ctx", route)


def local(query_mr, key_mr, value_mr, key_li, cotangent, norm_gain, filter_mr, filter_li):
    blocks = lax.axis_size("ctx")
    rows = query_mr.shape[0]
    short = short_tables()
    long = long_tables(blocks)
    width = rows // blocks
    gain = norm_gain.reshape(-1, LANES)
    moved_pair = swapped(pair_up(cotangent, filter_li, blocks)).reshape(2 * rows, LANES)
    prior = shifted(product_of(key_mr, value_mr), 1)
    grad_moved, cotan_spec = signal_grad(moved_pair, prior[:16], blocks, long)
    grad_signal = swapped(grad_moved)
    conv, mixed, window_spec, taps_spec, squares = mr_forward(
        key_mr, value_mr, prior, query_mr, filter_mr, grad_moved, short
    )
    squares = parts_over_ch(squares)
    grad_key_li, terms = mr_project(grad_signal, key_li, mixed, gain, squares)
    project = parts_over_ch(terms)
    taps_and_signal, spec = taps_grad_of(
        grad_signal, key_li, mixed, query_mr, gain, window_spec, short, project, squares, blocks
    )
    moved = swapped(taps_and_signal)
    grad_query, before_grad, own_grad = product_grad_of(
        grad_signal, key_li, mixed, conv, gain, spec, taps_spec, short, project, squares
    )
    after = shifted(before_grad, -1)
    grad_product = own_grad + after.astype(F32)
    grad_key = (grad_product * value_mr.astype(F32)).astype(BF16)
    grad_value = (grad_product * key_mr.astype(F32)).astype(BF16)
    bundled = filter_grad(moved, cotan_spec, grad_moved, after[:16], long)
    grad_filter_li, grad_filter_mr, gain_rows = deliver(swapped(bundled), gain, blocks, width)
    grad_gain = gain_rows.reshape(rows)
    return (
        grad_query,
        grad_key,
        grad_value,
        grad_key_li,
        grad_gain,
        grad_filter_mr,
        grad_filter_li,
    )


def solution(mesh):
    in_specs = (
        P("ch", "ctx"),
        P("ch", "ctx"),
        P("ch", "ctx"),
        P("ch", "ctx"),
        P("ch", "ctx"),
        P("ch"),
        P("ch", None),
        P("ch", "ctx"),
    )
    out_specs = (
        P("ch", "ctx"),
        P("ch", "ctx"),
        P("ch", "ctx"),
        P("ch", "ctx"),
        P("ch"),
        P("ch", None),
        P("ch", "ctx"),
    )
    return jax.shard_map(local, mesh=mesh, in_specs=in_specs, out_specs=out_specs, check_vma=False)
```
